32 devices in a mesh: grp: 2 (over y), pool: 4 (over z), head: 2 (over x), sub: 2 (over core).
Axes of the slice: x: 2, y: 2, z: 4, core: 2. Of those that a mesh axis runs over, the one named last changes fastest.
Arguments:
- pool: bfloat16 [192, 64, 576], P(('grp', 'pool')), parts along dimension 0, may hold values from -100 to 100
- block_table: int32 [16, 32], P(('grp', 'pool')), parts along dimension 0, may hold values from 0 to 95, as said below
- lengths: int32 [16], P(('grp', 'pool')), parts along dimension 0, may hold values from 1 to 2047, as said below
- new_slot: int32 [16], P(('grp', 'pool')), parts along dimension 0, may hold values from 0 to 7, each once
- q_nope: bfloat16 [16, 128, 128], P(('grp', 'pool'), ('head', 'sub')), parts along dimension 0, may hold values from -6 to 6
- q_rope: bfloat16 [16, 128, 64], P(('grp', 'pool'), ('head', 'sub')), parts along dimension 0, may hold values from -6 to 6
- new_latent: bfloat16 [16, 576], P(('grp', 'pool')), parts along dimension 0, may hold values from -700 to 700
- kv_gain: bfloat16 [512], replicated, may hold values from 0.5 to 1.5
- w_uk: bfloat16 [128, 128, 512], P(('head', 'sub')), may hold values from -0.5 to 0.5
- w_uv: bfloat16 [128, 512, 128], P(('head', 'sub')), may hold values from -0.25 to 0.25
Outputs:
- attn_out: bfloat16 [16, 128, 128], P(('grp', 'pool'), ('head', 'sub')), parts along dimension 0
- new_blocks: bfloat16 [16, 64, 576], P(('grp', 'pool'), ('head', 'sub')), parts along dimension 0
The draws below stay inside these ranges and needn't reach their ends.
There are 2 independent parts, one for each index of `grp`. The reference program is written for one: setup_inputs(seed, part) draws one part's arguments, and reference() takes and returns one part's arrays. A program takes and returns all parts, laid end to end along the dimension named above; an argument that names none is the same for every part. Nothing has to cross between parts.
Inputs may be any that keep to these rules, and one draw needn't show every extreme that they name: block_table[r, j] = o * 24 + s names slot s of owner o, where o = (block_table[r, 0] // 24 + j) mod 4 for every j; the blocks that hold positions below lengths[r] are distinct over all rows; entries for j at or beyond (lengths[r] + 63) // 64 are placeholders. `lengths`: exactly one row of a part has 2047. new_slot[r] = o * 2 + s returns row r's block to slot s of owner o; each value once.
All inputs are finite; a program needn't handle non-finite values.
Results may differ from the reference program's by a relative error of at most 0.0075.
Values may be sent and summed in bfloat16 or wider, within the bound.
No kernel may reach another device: no remote copies, remote signals or barrier semaphores. Data moves between devices by JAX's collectives and lax.ppermute only.
A program may use at most 64 MiB of HBM per device.

```python
import math
import jax
import jax.numpy as jnp
from jax import lax

HEADS = 128
NOPE = 128
ROPE = 64
KVL = 512
VDIM = 128
LAT = 576
BLOCK = 64
MAXBLK = 32
MAX_LEN = 2047
MEAN_LEN = 640
ROWS_DEV = 2
OWNERS = 4
ROWS = 8
SLOTS = 24
OWNER_SLOTS = 96


def layout(key):
    key = jax.random.fold_in(key, 101)
    subkeys = jax.random.split(key, 3)
    shares = jax.random.randint(subkeys[0], (ROWS,), 1, 65)
    weight = shares * shares
    spare_len = ROWS * MEAN_LEN - MAX_LEN
    lengths = 1 + weight * spare_len // jnp.sum(weight)
    lengths = jnp.minimum(lengths, MAX_LEN - 1)
    longest = jax.random.randint(subkeys[1], (), 0, ROWS)
    lengths = jnp.where(jnp.arange(ROWS) == longest, MAX_LEN, lengths).astype(jnp.int32)
    counts = (lengths + BLOCK - 1) // BLOCK
    starts = jnp.cumsum(counts) - counts
    global_order = starts[:, None] + jnp.arange(MAXBLK)[None, :]
    owners = ROWS // ROWS_DEV
    holder = global_order % owners
    local_index = global_order // owners % SLOTS
    shuffles = jax.vmap(lambda subkey: jax.random.permutation(subkey, SLOTS))(jax.random.split(subkeys[2], owners))
    slot_index = shuffles[holder, local_index]
    return (lengths, (holder * SLOTS + slot_index).astype(jnp.int32))


def draw_lengths(key, part):
    return layout(key)[0]


def draw_block_table(key, part):
    return layout(key)[1]


def draw_pool(key, part):
    key = jax.random.fold_in(key, 13)
    values = jnp.clip(jax.random.normal(key, (OWNER_SLOTS, BLOCK, LAT), jnp.float32), -6.0, 6.0)
    return values.astype(jnp.bfloat16)


def draw_q_rope(key, part):
    key = jax.random.fold_in(key, 7)
    values = jnp.clip(jax.random.normal(key, (ROWS, HEADS, ROPE), jnp.float32), -6.0, 6.0)
    return values.astype(jnp.bfloat16)


def draw_new_latent(key, part):
    key = jax.random.fold_in(key, 29)
    subkeys = jax.random.split(key, 3)
    values = jnp.clip(jax.random.normal(subkeys[0], (ROWS, LAT), jnp.float32), -6.0, 6.0)
    upper = 10.0
    row_scale = jnp.exp(jax.random.uniform(subkeys[1], (ROWS, 1), jnp.float32, 0.0, math.log(upper)))
    column_scale = jnp.exp(jax.random.uniform(subkeys[2], (1, KVL), jnp.float32, 0.0, math.log(upper)))
    scale_all = jnp.concatenate([row_scale * column_scale, jnp.ones((ROWS, ROPE), jnp.float32)], axis=1)
    return (values * scale_all).astype(jnp.bfloat16)


def steps_of(key, shape, cuts, least, top_value):
    def one(position, shards_of):
        steps = jax.random.uniform(jax.random.fold_in(jax.random.fold_in(key, 6), position), (shards_of,), jnp.float32, least / len(cuts), top_value / len(cuts))
        return jnp.repeat(jnp.exp(steps), shape[position] // shards_of).reshape((-1,) + (1,) * (len(shape) - position - 1))

    loudness = one(*cuts[0])
    for cut in cuts[1:]:
        loudness = loudness * one(*cut)
    return loudness


def gaussian(own_key, extent, width, bound, cuts=(), kind=jnp.bfloat16):
    entries = width * jax.random.normal(own_key, extent, jnp.float32)
    if cuts:
        entries = entries * steps_of(own_key, extent, cuts, -0.22, 0.18)
    return jnp.clip(entries, -bound, bound).astype(kind)


def setup_inputs(seed: int = 0, part: int = 0) -> dict:
    key_of = jax.random.split(jax.random.key(seed), 11)
    own_keys = jax.random.split(jax.random.fold_in(key_of[10], part), 11)
    return {
        "pool": draw_pool(jax.random.fold_in(jax.random.fold_in(key_of[10], part), 71), part),
        "block_table": draw_block_table(jax.random.fold_in(jax.random.fold_in(key_of[10], part), 71), part),
        "lengths": draw_lengths(jax.random.fold_in(jax.random.fold_in(key_of[10], part), 71), part),
        "new_slot": jax.random.permutation(own_keys[3], ROWS).astype(jnp.int32),
        "q_nope": gaussian(own_keys[4], (ROWS, HEADS, NOPE), 1.0, 6.0, ((0, 4), (1, 4))),
        "q_rope": draw_q_rope(jax.random.fold_in(jax.random.fold_in(key_of[10], part), 71), part),
        "new_latent": draw_new_latent(jax.random.fold_in(jax.random.fold_in(key_of[10], part), 71), part),
        "kv_gain": jnp.clip(1.0 + 0.1 * jax.random.normal(key_of[7], (KVL,), jnp.float32), 0.5, 1.5).astype(jnp.bfloat16),
        "w_uk": gaussian(key_of[8], (HEADS, NOPE, KVL), NOPE ** -0.5, 0.5, ((0, 4),)),
        "w_uv": gaussian(key_of[9], (HEADS, KVL, VDIM), KVL ** -0.5, 0.25, ((0, 4),)),
    }


EPS = 1e-06
SCALE = 192.0 ** (-0.5)

def rotate(values, positions):
    half_width = values.shape[-1] // 2
    frequency = 10000.0 ** (-jnp.arange(half_width, dtype=jnp.float32) / half_width)
    angles = positions.astype(jnp.float32)[..., None] * frequency
    cosine = jnp.cos(angles)
    sine_part = jnp.sin(angles)
    first_half = values[..., :half_width]
    second_half = values[..., half_width:]
    return jnp.concatenate([first_half * cosine - second_half * sine_part, second_half * cosine + first_half * sine_part], axis=-1)

def reference(pool, block_table, lengths, new_slot, q_nope, q_rope, new_latent, kv_gain, w_uk, w_uv):
    latent_raw = new_latent[:, :KVL].astype(jnp.float32)
    mean_square = lax.optimization_barrier(jnp.mean(latent_raw * latent_raw, axis=-1, keepdims=True))
    new_cache_lat = (latent_raw * lax.rsqrt(mean_square + EPS) * kv_gain.astype(jnp.float32)).astype(jnp.bfloat16)
    new_key = rotate(new_latent[:, KVL:].astype(jnp.float32), lengths)
    query_rot = rotate(q_rope.astype(jnp.float32), lengths[:, None])
    query_lat = jnp.einsum('rhn,hnl->rhl', q_nope.astype(jnp.float32), w_uk.astype(jnp.float32), precision=lax.Precision.HIGHEST).astype(jnp.bfloat16)

    def one_row(row_items):
        table_row, length, lat_row, rot_row, new_c_row, key_row = row_items
        row_keys = pool[table_row].reshape(MAXBLK * BLOCK, LAT)
        is_valid = jnp.arange(MAXBLK * BLOCK, dtype=jnp.int32) < length
        owner_of = jnp.repeat((table_row // SLOTS).astype(jnp.int32), BLOCK)
        one_hot = owner_of[None, :] == jnp.arange(OWNERS, dtype=jnp.int32)[:, None]
        scores = jnp.dot(lat_row, row_keys[:, :KVL].T, preferred_element_type=jnp.float32)
        scores = scores + jnp.dot(rot_row, row_keys[:, KVL:].astype(jnp.float32).T, precision=lax.Precision.HIGHEST)
        scores = SCALE * scores
        new_score = jnp.dot(lat_row, new_c_row, preferred_element_type=jnp.float32)
        new_score = SCALE * (new_score + jnp.dot(rot_row, key_row, precision=lax.Precision.HIGHEST))
        group_max = lax.optimization_barrier(jnp.max(jnp.where((one_hot & is_valid[None, :])[None], scores[:, None, :], -1e+30), axis=2))
        pos_max = group_max[:, owner_of]
        row_max = jnp.maximum(lax.optimization_barrier(jnp.max(group_max, axis=1)), new_score)
        weights = jnp.where(is_valid[None, :], jnp.exp(scores - pos_max), 0.0).astype(jnp.bfloat16)
        factor = jnp.exp(pos_max - row_max[:, None])
        scaled = weights.astype(jnp.float32) * factor
        new_weight = jnp.exp(new_score - row_max).astype(jnp.bfloat16)
        denominator = lax.optimization_barrier(jnp.sum(scaled, axis=1)) + new_weight.astype(jnp.float32)
        weighted = jnp.dot(scaled, row_keys[:, :KVL].astype(jnp.float32), precision=lax.Precision.HIGHEST)
        weighted = weighted + new_weight.astype(jnp.float32)[:, None] * new_c_row.astype(jnp.float32)[None, :]
        attended = (weighted / denominator[:, None]).astype(jnp.bfloat16)
        result = jnp.einsum('hl,hlv->hv', attended.astype(jnp.float32), w_uv.astype(jnp.float32), precision=lax.Precision.HIGHEST)
        return result.astype(jnp.bfloat16)
    attn_out = lax.map(one_row, (block_table, lengths, query_lat, query_rot, new_cache_lat, new_key))
    tail_index = lengths // BLOCK
    tail_block = jnp.take_along_axis(block_table, tail_index[:, None], axis=1)[:, 0]
    tail_rows = pool[tail_block]
    positions = BLOCK * tail_index[:, None] + jnp.arange(BLOCK, dtype=jnp.int32)[None, :]
    new_vector = jnp.concatenate([new_cache_lat, new_key.astype(jnp.bfloat16)], axis=1)
    block_rows = jnp.where((positions < lengths[:, None])[..., None], tail_rows, jnp.zeros_like(tail_rows))
    block_rows = jnp.where((positions == lengths[:, None])[..., None], new_vector[:, None, :], block_rows)
    new_blocks = jnp.zeros_like(block_rows).at[new_slot].set(block_rows)
    return (attn_out, new_blocks)
```

```python
import functools

import jax
import jax.numpy as jnp
import numpy as np
from jax import lax
from jax.experimental import pallas as pl
from jax.experimental.pallas import tpu as pltpu
from jax.sharding import PartitionSpec as P

EPS = 1e-06
SCALE = 192.0 ** (-0.5)
NONE = -1e30
BF = jnp.bfloat16
F32 = jnp.float32
LANES = 128
META = 32
NEW, TAIL_LEN, DEST, DEST_SLOT, COUNT = 0, 10, 12, 14, 16


def lane_ids(shape):
    return lax.broadcasted_iota(jnp.int32, shape, len(shape) - 1)


def row_ids(shape):
    return lax.broadcasted_iota(jnp.int32, shape, len(shape) - 2)


def rounded(values):
    return values.astype(BF).astype(F32)


def doubled(values):
    return jnp.concatenate([values, values], axis=-1)


def load_kernel(sources, targets, sems):
    copies = [
        pltpu.make_async_copy(source, target, sems.at[n])
        for n, (source, target) in enumerate(zip(sources, targets))
    ]
    for copy in copies:
        copy.start()
    for copy in copies:
        copy.wait()


def query_kernel(wide, *refs):
    sources = refs[:8]
    message, home = refs[8:10]
    targets = refs[10:18]
    meta, sems = refs[18:]
    load_kernel(sources, targets, sems)
    table, lengths, new_slot, q_nope, q_rope, new_latent, gain, freq = targets
    rows, heads, nope = q_nope.shape
    maxblk = table.shape[1]
    kvl = new_latent.shape[1] - q_rope.shape[2]
    queries = rows * heads
    whole = [q_nope[i].astype(F32) for i in range(rows)]

    lane = lane_ids((rows, LANES))
    row = row_ids((rows, LANES))
    position = jnp.full((rows, LANES), lengths[0], jnp.int32)
    for i in range(1, rows):
        position = jnp.where(row == i, lengths[i], position)
    angle = position.astype(F32) * freq[...]
    cosine = jnp.cos(angle)
    sine = jnp.sin(angle)
    sine = jnp.where(lane % 64 < 32, -sine, sine)
    qlane = lane_ids((heads, LANES))
    for i in range(rows):
        raw = doubled(q_rope[i].astype(F32))
        turned = raw * cosine[i : i + 1] + pltpu.roll(raw, 32, 1) * sine[i : i + 1]
        high = rounded(turned)
        whole.append(jnp.where(qlane < 64, high, turned - high))
    message[0 : 2 * queries, :] = jnp.concatenate(whole, axis=0).astype(BF)

    latent = new_latent[:, :kvl].astype(F32)
    square = jnp.mean(latent * latent, axis=-1, keepdims=True)
    gains = gain[...].astype(F32)
    gains = jnp.concatenate([gains[c : c + 1] for c in range(kvl // LANES)], axis=1)
    new_c = rounded(latent * lax.rsqrt(square + EPS) * gains)
    key = doubled(new_latent[:, kvl:].astype(F32))
    key = key * cosine + pltpu.roll(key, 32, 1) * sine
    home[...] = jnp.zeros_like(home)
    home[0:rows, 0:kvl] = new_c
    home[0:rows, kvl : kvl + LANES] = key
    meta[...] = jnp.zeros_like(meta)
    for c in range(kvl // LANES):
        meta[NEW + rows * c : NEW + rows * (c + 1), :] = new_c[:, c * LANES : (c + 1) * LANES]
    c = kvl // LANES
    meta[NEW + rows * c : NEW + rows * (c + 1), :] = key

    one = lane_ids((1, LANES))
    for i in range(rows):
        length = lengths[i]
        slot = new_slot[i]
        tail = table[i, length // 64]
        meta[TAIL_LEN + i : TAIL_LEN + i + 1, :] = jnp.full((1, LANES), length % 64, jnp.int32).astype(F32)
        meta[DEST + i : DEST + i + 1, :] = jnp.full((1, LANES), slot // rows, jnp.int32).astype(F32)
        meta[DEST_SLOT + i : DEST_SLOT + i + 1, :] = jnp.full((1, LANES), slot % rows, jnp.int32).astype(F32)
        counts = [jnp.zeros((1, LANES), jnp.int32) for _ in range(wide)]
        for j in range(maxblk):
            block = table[i, j]
            count = jnp.clip(length - 64 * j, 0, 64)
            for w in range(wide):
                counts[w] = counts[w] + jnp.where(one + w * LANES == block, count, 0)
        for w in range(wide):
            meta[COUNT + rows * w + i : COUNT + rows * w + i + 1, :] = counts[w].astype(F32)
            at = COUNT + rows * (wide + w) + i
            meta[at : at + 1, :] = jnp.where(one + w * LANES == tail, 1.0, 0.0)
    message[2 * queries : 2 * queries + META, :] = meta[...].astype(BF)


def attend_kernel(owners, head_parts, rows, heads, *refs):
    messages = refs[:owners]
    home, pool, w_uk, w_uv = refs[owners : owners + 4]
    replies = refs[owners + 4 : 2 * owners + 4]
    q_flat, lat, scores, out, meta = refs[2 * owners + 4 :]
    slots, block, width = pool.shape
    tokens = slots * block
    kvl = w_uk.shape[2]
    tiles = kvl // LANES
    queries = rows * heads
    everyone = owners * rows
    wide = (owners * slots + LANES - 1) // LANES
    me = lax.axis_index("pool")
    part = lax.axis_index(("head", "sub"))

    for k in range(owners):
        q_flat[k * queries : (k + 1) * queries, :] = messages[k][0:queries, :].astype(F32)
        meta[k] = messages[k][2 * queries : 2 * queries + META, :].astype(F32)

    for h in range(heads):
        one_head = q_flat[pl.ds(h, everyone, stride=heads), :].astype(BF)
        absorbed = jnp.dot(one_head, w_uk[h], preferred_element_type=F32)
        for c in range(tiles):
            lat[c, pl.ds(h, everyone, stride=heads), :] = absorbed[:, c * LANES : (c + 1) * LANES]

    lane = lane_ids((LANES, tokens))
    counts = jnp.zeros((everyone, tokens), F32)
    for w in range(wide):
        count_rows = jnp.concatenate(
            [meta[k, COUNT + rows * w : COUNT + rows * (w + 1), :] for k in range(owners)], axis=0
        ).astype(BF)
        here = jnp.where(
            row_ids((LANES, tokens)) + w * LANES == me * slots + lane // block, 1.0, 0.0
        ).astype(BF)
        counts = counts + jnp.dot(count_rows, here, preferred_element_type=F32)
    within = (lane_ids((everyone, tokens)) % block).astype(F32)
    bias = jnp.where(within < counts, 0.0, NONE)

    rotated = [messages[k][queries : 2 * queries, :] for k in range(owners)]
    turned = jnp.concatenate(rotated, axis=0) if owners > 1 else rotated[0]
    key_dims = (((1,), (1,)), ((), ()))
    flat_pool = pool[...].reshape(tokens, width)
    full = jnp.concatenate(
        [lat[c].astype(BF) for c in range(tiles)] + [turned[:, 0 : width - kvl]], axis=1
    )
    scores[...] = lax.dot_general(full, flat_pool, key_dims, preferred_element_type=F32)
    scores[...] += lax.dot_general(
        turned[:, width - kvl :], flat_pool[:, kvl:], key_dims, preferred_element_type=F32
    )

    own = rotated[0].astype(F32)
    biggest, totals, weights, new_weights = [], [], [], []
    for r in range(everyone):
        some = scores[r * heads : (r + 1) * heads, :] * SCALE + bias[r : r + 1, :]
        top = jnp.max(some, axis=1, keepdims=True)
        if r < rows:
            new_score = jnp.zeros((heads, LANES), F32)
            for c in range(tiles):
                mine = rounded(lat[c, r * heads : (r + 1) * heads, :])
                new_score = new_score + mine * home[r : r + 1, c * LANES : (c + 1) * LANES]
            new_score = jnp.sum(new_score, axis=1, keepdims=True)
            both = own[r * heads : (r + 1) * heads, :]
            both = both + pltpu.roll(both, 64, 1)
            new_score = SCALE * (
                new_score
                + 0.5 * jnp.sum(both * home[r : r + 1, kvl : kvl + LANES], axis=1, keepdims=True)
            )
            top = jnp.maximum(top, new_score)
        weight = jnp.exp(some - top).astype(BF)
        total = jnp.sum(weight.astype(F32), axis=1, keepdims=True)
        if r < rows:
            new_weight = rounded(jnp.exp(new_score - top))
            total = total + new_weight
            new_weights.append(new_weight)
        else:
            total = jnp.where(top > 0.5 * NONE, total, 0.0)
        biggest.append(top)
        totals.append(total)
        weights.append(weight)
    values = flat_pool[:, :kvl]
    sums = jnp.dot(jnp.concatenate(weights, axis=0), values, preferred_element_type=F32)
    for r in range(everyone):
        some = sums[r * heads : (r + 1) * heads, :]
        if r < rows:
            some = some + new_weights[r] * home[r : r + 1, 0:kvl]
        share = jnp.where(totals[r] > 0.0, 1.0 / jnp.maximum(totals[r], 1e-30), 0.0)
        some = some * share
        for c in range(tiles):
            lat[c, r * heads : (r + 1) * heads, :] = some[:, c * LANES : (c + 1) * LANES]

    for h in range(heads):
        one_head = jnp.concatenate(
            [lat[c, pl.ds(h, everyone, stride=heads), :] for c in range(tiles)], axis=1
        ).astype(BF)
        out[pl.ds(h, everyone, stride=heads), :] = jnp.dot(
            one_head, w_uv[h], preferred_element_type=F32
        )

    span = block // head_parts
    tails = everyone * span
    if span % 16 == 0:
        near_span, first = span, part * span
        near_pool = pool[:, pl.ds(pl.multiple_of(first, span), span), :]
        near_pool = near_pool.reshape(slots * span, width)
    else:
        near_span, first = block, 0
        near_pool = flat_pool
    near = slots * near_span
    where_from = first + lane_ids((1, near)) % near_span
    place = row_ids((tails, near))
    diagonal = part * span + place % span == first + lane_ids((tails, near)) % near_span
    chosen = jnp.zeros((tails, near), F32)
    new_rows = [jnp.zeros((tails, LANES), F32) for _ in range(kvl // LANES + 1)]
    token = part * span + row_ids((tails, LANES)) % span
    for k in range(owners):
        dest = meta[k, DEST : DEST + rows, :]
        dest = me.astype(F32) - dest
        dest = jnp.where(dest < 0.0, dest + owners, dest)
        dest = dest * rows + meta[k, DEST_SLOT : DEST_SLOT + rows, :]
        tail_len = meta[k, TAIL_LEN : TAIL_LEN + rows, :]
        is_last = jnp.zeros((rows, near), F32)
        for w in range(wide):
            here = jnp.where(
                row_ids((LANES, near)) + w * LANES == me * slots + lane_ids((LANES, near)) // near_span,
                1.0,
                0.0,
            ).astype(BF)
            at = COUNT + rows * (wide + w)
            is_last = is_last + jnp.dot(
                meta[k, at : at + rows, :].astype(BF), here, preferred_element_type=F32
            )
        is_holder = jnp.max(is_last, axis=1, keepdims=True)
        for i in range(rows):
            old = jnp.where(
                where_from.astype(F32) < tail_len[i : i + 1, 0:1],
                is_last[i : i + 1, :],
                0.0,
            )
            goes = (place // span).astype(F32) == dest[i : i + 1, 0:1]
            chosen = chosen + jnp.where(goes, old, 0.0)
            new_here = (
                ((row_ids((tails, LANES)) // span).astype(F32) == dest[i : i + 1, :])
                & (token.astype(F32) == tail_len[i : i + 1, :])
                & (is_holder[i : i + 1, :] > 0.5)
            )
            for c in range(kvl // LANES + 1):
                new_rows[c] = new_rows[c] + jnp.where(
                    new_here, meta[k, NEW + rows * c + i : NEW + rows * c + i + 1, :], 0.0
                )
    chosen = jnp.where(diagonal, chosen, 0.0).astype(BF)
    tail_rows = jnp.dot(chosen, near_pool, preferred_element_type=F32)

    send_lane = lane_ids((heads, LANES))
    tail_lane = lane_ids((rows * span, LANES))
    for k in range(owners):
        mine = slice(k * rows * span, (k + 1) * rows * span)
        whole = [out[k * queries : (k + 1) * queries, :]]
        for c in range(tiles):
            whole.append(tail_rows[mine, c * LANES : (c + 1) * LANES] + new_rows[c][mine, :])
        last = doubled(tail_rows[mine, kvl:]) + new_rows[tiles][mine, :]
        stats = jnp.zeros((heads, LANES), F32)
        for i in range(rows):
            for n, value in enumerate((biggest[k * rows + i], totals[k * rows + i])):
                for piece in range(3):
                    high = rounded(value)
                    stats = jnp.where(send_lane == 64 + 6 * i + 3 * n + piece, high, stats)
                    value = value - high
        whole.append(jnp.where(tail_lane < 64, last, stats))
        whole = jnp.concatenate(whole, axis=0)
        missing = replies[k].shape[0] - whole.shape[0]
        if missing:
            whole = jnp.concatenate([whole, jnp.zeros((missing, LANES), F32)], axis=0)
        replies[k][...] = whole.astype(BF)


def combine_kernel(rows, heads, span, *refs):
    replies = [reply[...].astype(F32) for reply in refs[:-2]]
    attn_out, new_blocks = refs[-2:]
    kvl_tiles = new_blocks.shape[2] // LANES
    queries = rows * heads
    last = queries + kvl_tiles * rows * span
    stats = [reply[last : last + heads, :] for reply in replies]
    for i in range(rows):
        tops, totals = [], []
        for stat in stats:
            at = 64 + 6 * i
            tops.append(stat[:, at : at + 1] + stat[:, at + 1 : at + 2] + stat[:, at + 2 : at + 3])
            at = at + 3
            totals.append(stat[:, at : at + 1] + stat[:, at + 1 : at + 2] + stat[:, at + 2 : at + 3])
        top = functools.reduce(jnp.maximum, tops)
        shares = [jnp.exp(t - top) * total for t, total in zip(tops, totals)]
        denominator = functools.reduce(jnp.add, shares)
        result = jnp.zeros((heads, LANES), F32)
        for share, reply in zip(shares, replies):
            result = result + share * reply[i * heads : (i + 1) * heads, :]
        attn_out[i] = (result / denominator).astype(BF)
    for c in range(kvl_tiles + 1):
        at = queries + c * rows * span
        tile = replies[0][at : at + rows * span, :]
        for reply in replies[1:]:
            tile = tile + reply[at : at + rows * span, :]
        left = min(LANES, new_blocks.shape[2] - c * LANES)
        for i in range(rows):
            new_blocks[i, :, c * LANES : c * LANES + left] = tile[
                i * span : (i + 1) * span, 0:left
            ].astype(BF)


def per_device(
    pool, block_table, lengths, new_slot, q_nope, q_rope, new_latent, kv_gain, w_uk, w_uv
):
    owners = lax.axis_size("pool")
    parts = lax.axis_size(("head", "sub"))
    slots, block, width = pool.shape
    rows, heads, nope = q_nope.shape
    rope = q_rope.shape[2]
    kvl = kv_gain.shape[0]
    vdim = w_uv.shape[2]
    queries = rows * heads
    everyone = owners * rows
    wide = (owners * slots + LANES - 1) // LANES
    span = block // parts
    tokens = slots * block
    vmem = pl.BlockSpec(memory_space=pltpu.VMEM)
    hbm = pl.BlockSpec(memory_space=pltpu.HBM)

    half = rope // 2
    freq = 10000.0 ** (-(np.arange(LANES) % half).astype(np.float32) / np.float32(half))
    freq = jnp.asarray(freq.astype(np.float32)[None])
    gain = kv_gain.reshape(-1, LANES)
    raw = (block_table, lengths, new_slot, q_nope, q_rope, new_latent, gain, freq)
    raw = [pltpu.with_memory_space_constraint(a, pltpu.HBM) for a in raw]
    message, home = pl.pallas_call(
        functools.partial(query_kernel, wide),
        out_shape=(
            pltpu.VMEM((2 * queries + META, LANES), BF),
            pltpu.VMEM((8, kvl + LANES), F32),
        ),
        in_specs=[hbm] * len(raw),
        out_specs=(vmem, vmem),
        scratch_shapes=[
            (pltpu.SMEM if n < 3 else pltpu.VMEM)(a.shape, a.dtype) for n, a in enumerate(raw)
        ]
        + [pltpu.VMEM((META, LANES), F32), pltpu.SemaphoreType.DMA((len(raw),))],
        compiler_params=pltpu.CompilerParams(vmem_limit_bytes=4 * 2**20),
        name="queries",
    )(*raw)

    def ring(step):
        return [(i, (i + step) % owners) for i in range(owners)]

    messages = [message]
    for k in range(1, owners):
        messages.append(lax.ppermute(message, "pool", ring(k)))

    near = pl.pallas_call(
        lambda *refs: load_kernel(refs[:3], refs[3:6], refs[6]),
        out_shape=tuple(pltpu.VMEM(a.shape, a.dtype) for a in (w_uk, pool, w_uv)),
        in_specs=[hbm] * 3,
        out_specs=(vmem,) * 3,
        scratch_shapes=[pltpu.SemaphoreType.DMA((3,))],
        compiler_params=pltpu.CompilerParams(vmem_limit_bytes=2**20),
        cost_estimate=pl.CostEstimate(flops=0, bytes_accessed=20 * 2**20, transcendentals=0),
        name="load",
    )(*[pltpu.with_memory_space_constraint(a, pltpu.HBM) for a in (w_uk, pool, w_uv)])

    reply_rows = -(-(queries + (kvl // LANES + 1) * rows * span) // 16) * 16
    replies = pl.pallas_call(
        functools.partial(attend_kernel, owners, parts, rows, heads),
        out_shape=tuple(
            jax.ShapeDtypeStruct((reply_rows, LANES), BF) for _ in range(owners)
        ),
        in_specs=[vmem] * (owners + 4),
        out_specs=tuple([vmem] * owners),
        scratch_shapes=[
            pltpu.VMEM((owners * queries, nope), F32),
            pltpu.VMEM((kvl // LANES, owners * queries, LANES), F32),
            pltpu.VMEM((owners * queries, tokens), F32),
            pltpu.VMEM((owners * queries, vdim), F32),
            pltpu.VMEM((owners, META, LANES), F32),
        ],
        compiler_params=pltpu.CompilerParams(vmem_limit_bytes=24 * 2**20),
        name="attend",
    )(*messages, home, near[1], near[0], near[2])

    returned = [replies[0]]
    for k in range(1, owners):
        returned.append(lax.ppermute(replies[k], "pool", ring(-k)))

    return pl.pallas_call(
        functools.partial(combine_kernel, rows, heads, span),
        out_shape=(
            jax.ShapeDtypeStruct((rows, heads, vdim), BF),
            jax.ShapeDtypeStruct((rows, span, width), BF),
        ),
        in_specs=[vmem] * owners,
        out_specs=(vmem, vmem),
        compiler_params=pltpu.CompilerParams(vmem_limit_bytes=4 * 2**20),
        name="combine",
    )(*returned)


def solution(mesh):
    placed = (
        P(("grp", "pool"), None, None),
        P(("grp", "pool"), None),
        P(("grp", "pool")),
        P(("grp", "pool")),
        P(("grp", "pool"), ("head", "sub"), None),
        P(("grp", "pool"), ("head", "sub"), None),
        P(("grp", "pool"), None),
        P(),
        P(("head", "sub"), None, None),
        P(("head", "sub"), None, None),
    )
    return jax.shard_map(
        per_device,
        mesh=mesh,
        in_specs=placed,
        out_specs=(
            P(("grp", "pool"), ("head", "sub"), None),
            P(("grp", "pool"), ("head", "sub"), None),
        ),
        check_vma=False,
    )
```

```python
import functools

import jax
import jax.numpy as jnp
import numpy as np
from jax import lax
from jax.experimental import pallas as pl
from jax.experimental.pallas import tpu as pltpu
from jax.sharding import PartitionSpec as P

EPS = 1e-06
SCALE = 192.0 ** (-0.5)
NONE = -1e30
BF = jnp.bfloat16
F32 = jnp.float32
LANES = 128
META = 32
NEW, TAIL_LEN, DEST, DEST_SLOT, COUNT = 0, 5, 6, 7, 8
LOG2E = 1.4426950408889634
ABSORB_UNROLL, SOFTEN_UNROLL, PROJECT_UNROLL = 32, 16, 32


def lane_ids(shape):
    return lax.broadcasted_iota(jnp.int32, shape, len(shape) - 1)


def row_ids(shape):
    return lax.broadcasted_iota(jnp.int32, shape, len(shape) - 2)


def rounded(values):
    return values.astype(BF).astype(F32)


def doubled(values):
    return jnp.concatenate([values, values], axis=-1)


def each_of(count, unroll, body):
    unroll = min(count, unroll)
    if unroll == count:
        for n in range(count):
            body(n)
    else:

        def some(n, carry):
            for m in range(unroll):
                body(n * unroll + m)
            return carry

        lax.fori_loop(0, count // unroll, some, 0)


def copies_of(sources, targets, sems, pieces=1):
    copies = []
    for source, target in zip(sources, targets):
        size = source.shape[0] // pieces
        for n in range(pieces):
            part = pl.ds(n * size, size)
            copies.append(
                pltpu.make_async_copy(source.at[part], target.at[part], sems.at[len(copies)])
            )
    for copy in copies:
        copy.start()
    return copies


def load_kernel(w_uk_hbm, pool_hbm, w_uk, pool, sems):
    for copy in copies_of([w_uk_hbm, pool_hbm], [w_uk, pool], sems, 4):
        copy.wait()


def query_kernel(wide, *refs):
    sources = refs[:8]
    message, home = refs[8:10]
    targets = refs[10:18]
    meta, sems = refs[18:]
    copies = copies_of(sources, targets, sems)
    for copy in copies:
        copy.wait()
    table, lengths, new_slot, q_nope, q_rope, new_latent, gain, freq = targets
    rows, heads, nope = q_nope.shape
    maxblk = table.shape[1]
    kvl = new_latent.shape[1] - q_rope.shape[2]
    queries = rows * heads
    whole = [q_nope[i].astype(F32) for i in range(rows)]

    lane = lane_ids((rows, LANES))
    row = row_ids((rows, LANES))
    position = jnp.full((rows, LANES), lengths[0], jnp.int32)
    for i in range(1, rows):
        position = jnp.where(row == i, lengths[i], position)
    angle = position.astype(F32) * freq[...]
    cosine = jnp.cos(angle)
    sine = jnp.sin(angle)
    sine = jnp.where(lane % 64 < 32, -sine, sine)
    qlane = lane_ids((heads, LANES))
    for i in range(rows):
        raw = doubled(q_rope[i].astype(F32))
        turned = raw * cosine[i : i + 1] + pltpu.roll(raw, 32, 1) * sine[i : i + 1]
        high = rounded(turned)
        whole.append(jnp.where(qlane < 64, high, turned - high))
    message[0 : 2 * queries, :] = jnp.concatenate(whole, axis=0).astype(BF)

    latent = new_latent[:, :kvl].astype(F32)
    square = jnp.mean(latent * latent, axis=-1, keepdims=True)
    gains = gain[...].astype(F32)
    gains = jnp.concatenate([gains[c : c + 1] for c in range(kvl // LANES)], axis=1)
    new_c = rounded(latent * lax.rsqrt(square + EPS) * gains)
    key = doubled(new_latent[:, kvl:].astype(F32))
    key = key * cosine + pltpu.roll(key, 32, 1) * sine
    home[...] = jnp.zeros_like(home)
    home[0:rows, 0:kvl] = new_c
    home[0:rows, kvl : kvl + LANES] = key
    meta[...] = jnp.zeros_like(meta)
    for c in range(kvl // LANES):
        meta[rows * (NEW + c) : rows * (NEW + c + 1), :] = new_c[:, c * LANES : (c + 1) * LANES]
    c = kvl // LANES
    meta[rows * (NEW + c) : rows * (NEW + c + 1), :] = key

    one = lane_ids((1, LANES))
    for i in range(rows):
        length = lengths[i]
        slot = new_slot[i]
        tail = table[i, length // 64]
        for n, value in ((TAIL_LEN, length % 64), (DEST, slot // rows), (DEST_SLOT, slot % rows)):
            at = rows * n + i
            meta[at : at + 1, :] = jnp.full((1, LANES), value, jnp.int32).astype(F32)
        counts = [jnp.zeros((1, LANES), jnp.int32) for _ in range(wide)]
        for j in range(maxblk):
            block = table[i, j]
            count = jnp.clip(length - 64 * j, 0, 64)
            for w in range(wide):
                counts[w] = counts[w] + jnp.where(one + w * LANES == block, count, 0)
        for w in range(wide):
            at = rows * (COUNT + w) + i
            meta[at : at + 1, :] = counts[w].astype(F32)
            at = rows * (COUNT + wide + w) + i
            meta[at : at + 1, :] = jnp.where(one + w * LANES == tail, 1.0, 0.0)
    message[2 * queries : 2 * queries + META, :] = meta[...].astype(BF)


def attend_kernel(owners, head_parts, rows, heads, *refs):
    messages = refs[:owners]
    home, w_uk, pool, w_uv_hbm = refs[owners : owners + 4]
    replies = refs[owners + 4 : 2 * owners + 4]
    w_uv, q_flat, lat, scores, weights, out, each, bias, tops, totals, new_scores, sems = refs[
        2 * owners + 4 :
    ]
    w_uv_copies = copies_of([w_uv_hbm], [w_uv], sems, 1)
    slots, block, width = pool.shape
    tokens = slots * block
    kvl = w_uk.shape[2]
    tiles = kvl // LANES
    queries = rows * heads
    everyone = owners * rows
    wide = (owners * slots + LANES - 1) // LANES
    me = lax.axis_index("pool")
    part = lax.axis_index(("head", "sub"))

    for k in range(owners):
        q_flat[k * queries : (k + 1) * queries, :] = messages[k][0:queries, :].astype(F32)
        told = messages[k][2 * queries : 2 * queries + META, :].astype(F32)
        for n in range(each.shape[0]):
            each[n, rows * k : rows * (k + 1), :] = told[rows * n : rows * (n + 1), :]

    def absorb(h):
        one_head = q_flat[pl.ds(h, everyone, stride=heads), :].astype(BF)
        absorbed = jnp.dot(one_head, w_uk[h], preferred_element_type=F32)
        for c in range(tiles):
            lat[c, pl.ds(h, everyone, stride=heads), :] = absorbed[:, c * LANES : (c + 1) * LANES]

    each_of(heads, ABSORB_UNROLL, absorb)

    lane = lane_ids((LANES, tokens))
    counts = jnp.zeros((everyone, tokens), F32)
    for w in range(wide):
        here = jnp.where(
            row_ids((LANES, tokens)) + w * LANES == me * slots + lane // block, 1.0, 0.0
        ).astype(BF)
        counts = counts + jnp.dot(each[COUNT + w].astype(BF), here, preferred_element_type=F32)
    within = (lane_ids((everyone, tokens)) % block).astype(F32)
    bias[...] = jnp.where(within < counts, 0.0, NONE)

    turned = jnp.concatenate(
        [messages[k][queries : 2 * queries, :] for k in range(owners)], axis=0
    )
    flat_pool = pool[...].reshape(tokens, width)
    full = jnp.concatenate([lat[c].astype(BF) for c in range(tiles)] + [turned], axis=1)
    keys = jnp.concatenate([flat_pool, flat_pool[:, kvl:]], axis=1)
    scores[...] = lax.dot_general(
        full, keys, (((1,), (1,)), ((), ())), preferred_element_type=F32
    )

    new_score = jnp.zeros((queries, LANES), F32)
    new_c = []
    for c in range(tiles):
        new_c.append(
            jnp.concatenate(
                [
                    jnp.broadcast_to(
                        home[r : r + 1, c * LANES : (c + 1) * LANES], (heads, LANES)
                    )
                    for r in range(rows)
                ],
                axis=0,
            )
        )
        new_score = new_score + rounded(lat[c, 0:queries, :]) * new_c[c]
    both = messages[0][queries : 2 * queries, :].astype(F32)
    both = both + pltpu.roll(both, 64, 1)
    new_key = jnp.concatenate(
        [
            jnp.broadcast_to(home[r : r + 1, kvl : kvl + LANES], (heads, LANES))
            for r in range(rows)
        ],
        axis=0,
    )
    new_score = new_score + 0.5 * both * new_key
    new_score = jnp.sum(new_score, axis=1, keepdims=True) * (SCALE * LOG2E)
    new_scores[...] = jnp.full(new_scores.shape, NONE, F32)
    new_scores[0:queries, :] = jnp.broadcast_to(new_score, (queries, LANES))

    chunk = 16

    def soften(n):
        at = pl.ds(pl.multiple_of(n * chunk, chunk), chunk)
        if heads >= chunk:
            shown = bias[pl.ds(n * chunk // heads, 1), :]
        else:
            shown = [bias[pl.ds(n * (chunk // heads) + m, 1), :] for m in range(chunk // heads)]
            shown = [jnp.broadcast_to(one, (heads, tokens)) for one in shown]
            shown = jnp.concatenate(shown, axis=0)
        some = scores[at, :] * (SCALE * LOG2E) + shown
        new = new_scores[at, 0:1]
        top = jnp.maximum(jnp.max(some, axis=1, keepdims=True), new)
        weight = jnp.exp2(some - top).astype(BF)
        weights[at, :] = weight
        total = jnp.sum(weight.astype(F32), axis=1, keepdims=True)
        total = jnp.where(top > 0.5 * NONE, total + rounded(jnp.exp2(new - top)), 0.0)
        tops[at, :] = jnp.broadcast_to(top, (chunk, LANES))
        totals[at, :] = jnp.broadcast_to(total, (chunk, LANES))

    each_of(owners * queries // chunk, SOFTEN_UNROLL, soften)
    sums = jnp.dot(weights[...], flat_pool[:, :kvl], preferred_element_type=F32)
    share = jnp.where(totals[...] > 0.0, 1.0 / jnp.maximum(totals[...], 1e-30), 0.0)
    new_weight = rounded(jnp.exp2(new_scores[0:queries, :] - tops[0:queries, :]))
    for c in range(tiles):
        some = sums[:, c * LANES : (c + 1) * LANES]
        lat[c, 0:queries, :] = (some[0:queries] + new_weight * new_c[c]) * share[0:queries]
        lat[c, queries:, :] = some[queries:] * share[queries:]

    for copy in w_uv_copies:
        copy.wait()

    def project(h):
        one_head = jnp.concatenate(
            [lat[c, pl.ds(h, everyone, stride=heads), :] for c in range(tiles)], axis=1
        ).astype(BF)
        out[pl.ds(h, everyone, stride=heads), :] = jnp.dot(
            one_head, w_uv[h], preferred_element_type=F32
        )

    each_of(heads, PROJECT_UNROLL, project)

    span = block // head_parts
    tails = everyone * span
    if span % 16 == 0:
        near_span, first = span, part * span
        near_pool = pool[:, pl.ds(pl.multiple_of(first, span), span), :]
        near_pool = near_pool.reshape(slots * span, width)
    else:
        near_span, first = block, 0
        near_pool = flat_pool
    near = slots * near_span
    dest = (each[DEST].astype(jnp.int32) ^ me) * rows + each[DEST_SLOT].astype(jnp.int32)
    dest = jnp.concatenate([dest] * (tails // LANES), axis=1)
    goes = jnp.where(dest == lane_ids((everyone, tails)) // span, 1.0, 0.0).astype(BF)
    facts = [each[COUNT + wide + w] for w in range(wide)] + [each[TAIL_LEN]]
    facts = jnp.concatenate(facts + [each[NEW + c] for c in range(tiles + 1)], axis=1).astype(BF)
    facts = lax.dot_general(goes, facts, (((0,), (0,)), ((), ())), preferred_element_type=F32)
    is_last = facts[:, 0 : wide * LANES].astype(BF)
    tail_len = facts[:, wide * LANES : (wide + 1) * LANES]
    new_rows = facts[:, (wide + 1) * LANES :]
    pool_row = row_ids((wide * LANES, near + LANES)) - me * slots
    pool_lane = lane_ids((wide * LANES, near + LANES))
    here = (pool_row == pool_lane // near_span) & (pool_lane < near)
    here = here | ((pool_lane >= near) & (pool_row >= 0) & (pool_row < slots))
    chosen = jnp.dot(
        is_last, jnp.where(here, 1.0, 0.0).astype(BF), preferred_element_type=F32
    )
    is_holder = chosen[:, near:] > 0.5
    token = (part * span + row_ids((tails, LANES)) % span).astype(F32)
    place = row_ids((tails, near))
    diagonal = part * span + place % span == first + lane_ids((tails, near)) % near_span
    is_old = jnp.concatenate([token < tail_len] * (near // LANES), axis=1)
    chosen = jnp.where(diagonal & is_old, chosen[:, :near], 0.0).astype(BF)
    tail_rows = jnp.dot(chosen, near_pool, preferred_element_type=F32)
    tail_rows = jnp.concatenate([tail_rows, tail_rows[:, kvl:]], axis=1)
    is_new = is_holder & (token == tail_len)

    lane = lane_ids((heads, LANES))
    tail_lane = lane_ids((rows * span, LANES))
    for k in range(owners):
        mine = slice(k * rows * span, (k + 1) * rows * span)
        whole = [out[k * queries : (k + 1) * queries, :]]
        for c in range(tiles + 1):
            at = slice(c * LANES, (c + 1) * LANES)
            whole.append(tail_rows[mine, at] + jnp.where(is_new[mine], new_rows[mine, at], 0.0))
        stats = jnp.zeros((heads, LANES), F32)
        for i in range(rows):
            r = k * rows + i
            total = totals[r * heads : (r + 1) * heads, :]
            value = tops[r * heads : (r + 1) * heads, :] + jnp.log2(jnp.maximum(total, 1e-30))
            value = jnp.where(total > 0.0, value, NONE)
            for piece in range(3):
                high = rounded(value)
                stats = jnp.where(lane == 64 + 3 * i + piece, high, stats)
                value = value - high
        whole[-1] = jnp.where(tail_lane < 64, whole[-1], stats)
        whole = jnp.concatenate(whole, axis=0)
        missing = replies[k].shape[0] - whole.shape[0]
        if missing:
            whole = jnp.concatenate([whole, jnp.zeros((missing, LANES), F32)], axis=0)
        replies[k][...] = whole.astype(BF)


def combine_kernel(rows, heads, span, *refs):
    replies = [reply[...].astype(F32) for reply in refs[:-2]]
    attn_out, new_blocks = refs[-2:]
    kvl_tiles = new_blocks.shape[2] // LANES
    queries = rows * heads
    last = queries + kvl_tiles * rows * span
    stats = [reply[last : last + heads, :] for reply in replies]
    for i in range(rows):
        at = 64 + 3 * i
        sizes = [
            stat[:, at : at + 1] + stat[:, at + 1 : at + 2] + stat[:, at + 2 : at + 3]
            for stat in stats
        ]
        top = functools.reduce(jnp.maximum, sizes)
        shares = [jnp.exp2(size - top) for size in sizes]
        denominator = functools.reduce(jnp.add, shares)
        result = jnp.zeros((heads, LANES), F32)
        for share, reply in zip(shares, replies):
            result = result + share * reply[i * heads : (i + 1) * heads, :]
        attn_out[i] = (result / denominator).astype(BF)
    for c in range(kvl_tiles + 1):
        at = queries + c * rows * span
        tile = replies[0][at : at + rows * span, :]
        for reply in replies[1:]:
            tile = tile + reply[at : at + rows * span, :]
        left = min(LANES, new_blocks.shape[2] - c * LANES)
        for i in range(rows):
            new_blocks[i, :, c * LANES : c * LANES + left] = tile[
                i * span : (i + 1) * span, 0:left
            ].astype(BF)


def swap_order(owners):
    steps = list(range(1, owners))
    return [k for k in steps if k % 2] + [k for k in steps if k % 2 == 0]


def per_device(
    pool, block_table, lengths, new_slot, q_nope, q_rope, new_latent, kv_gain, w_uk, w_uv
):
    owners = lax.axis_size("pool")
    parts = lax.axis_size(("head", "sub"))
    slots, block, width = pool.shape
    rows, heads, nope = q_nope.shape
    rope = q_rope.shape[2]
    kvl = kv_gain.shape[0]
    vdim = w_uv.shape[2]
    queries = rows * heads
    everyone = owners * rows
    wide = (owners * slots + LANES - 1) // LANES
    span = block // parts
    tokens = slots * block
    vmem = pl.BlockSpec(memory_space=pltpu.VMEM)
    hbm = pl.BlockSpec(memory_space=pltpu.HBM)

    half = rope // 2
    freq = 10000.0 ** (-(np.arange(LANES) % half).astype(np.float32) / np.float32(half))
    freq = jnp.asarray(freq.astype(np.float32)[None])
    gain = kv_gain.reshape(-1, LANES)
    raw = (block_table, lengths, new_slot, q_nope, q_rope, new_latent, gain, freq)
    raw = [pltpu.with_memory_space_constraint(a, pltpu.HBM) for a in raw]
    message, home = pl.pallas_call(
        functools.partial(query_kernel, wide),
        out_shape=(
            pltpu.VMEM((2 * queries + META, LANES), BF),
            pltpu.VMEM((8, kvl + LANES), F32),
        ),
        in_specs=[hbm] * len(raw),
        out_specs=(vmem, vmem),
        scratch_shapes=[
            (pltpu.SMEM if n < 3 else pltpu.VMEM)(a.shape, a.dtype) for n, a in enumerate(raw)
        ]
        + [pltpu.VMEM((META, LANES), F32), pltpu.SemaphoreType.DMA((len(raw),))],
        compiler_params=pltpu.CompilerParams(vmem_limit_bytes=4 * 2**20),
        name="queries",
    )(*raw)

    def swap(array, k):
        return lax.ppermute(array, "pool", [(i, i ^ k) for i in range(owners)])

    order = swap_order(owners)
    messages = [message] + [None] * (owners - 1)
    for k in order:
        messages[k] = swap(message, k)

    pool, w_uk, w_uv = [
        pltpu.with_memory_space_constraint(a, pltpu.HBM) for a in (pool, w_uk, w_uv)
    ]
    w_uk, pool = pl.pallas_call(
        load_kernel,
        out_shape=(pltpu.VMEM(w_uk.shape, BF), pltpu.VMEM(pool.shape, BF)),
        in_specs=[hbm] * 2,
        out_specs=(vmem, vmem),
        scratch_shapes=[pltpu.SemaphoreType.DMA((8,))],
        compiler_params=pltpu.CompilerParams(vmem_limit_bytes=2**20),
        cost_estimate=pl.CostEstimate(flops=0, bytes_accessed=20 * 2**20, transcendentals=0),
        name="load",
    )(w_uk, pool)

    reply_rows = -(-(queries + (kvl // LANES + 1) * rows * span) // 16) * 16
    replies = pl.pallas_call(
        functools.partial(attend_kernel, owners, parts, rows, heads),
        out_shape=tuple(
            jax.ShapeDtypeStruct((reply_rows, LANES), BF) for _ in range(owners)
        ),
        in_specs=[vmem] * (owners + 3) + [hbm],
        out_specs=tuple([vmem] * owners),
        scratch_shapes=[
            pltpu.VMEM(w_uv.shape, BF),
            pltpu.VMEM((owners * queries, nope), F32),
            pltpu.VMEM((kvl // LANES, owners * queries, LANES), F32),
            pltpu.VMEM((owners * queries, tokens), F32),
            pltpu.VMEM((owners * queries, tokens), BF),
            pltpu.VMEM((owners * queries, vdim), F32),
            pltpu.VMEM((COUNT + 2 * wide, everyone, LANES), F32),
            pltpu.VMEM((everyone, tokens), F32),
            pltpu.VMEM((owners * queries, LANES), F32),
            pltpu.VMEM((owners * queries, LANES), F32),
            pltpu.VMEM((owners * queries, LANES), F32),
            pltpu.SemaphoreType.DMA((1,)),
        ],
        compiler_params=pltpu.CompilerParams(vmem_limit_bytes=24 * 2**20),
        name="attend",
    )(*messages, home, w_uk, pool, w_uv)

    returned = [replies[0]] + [None] * (owners - 1)
    for k in order:
        returned[k] = swap(replies[k], k)

    return pl.pallas_call(
        functools.partial(combine_kernel, rows, heads, span),
        out_shape=(
            jax.ShapeDtypeStruct((rows, heads, vdim), BF),
            jax.ShapeDtypeStruct((rows, span, width), BF),
        ),
        in_specs=[vmem] * owners,
        out_specs=(vmem, vmem),
        compiler_params=pltpu.CompilerParams(vmem_limit_bytes=4 * 2**20),
        name="combine",
    )(*returned)


def solution(mesh):
    placed = (
        P(("grp", "pool"), None, None),
        P(("grp", "pool"), None),
        P(("grp", "pool")),
        P(("grp", "pool")),
        P(("grp", "pool"), ("head", "sub"), None),
        P(("grp", "pool"), ("head", "sub"), None),
        P(("grp", "pool"), None),
        P(),
        P(("head", "sub"), None, None),
        P(("head", "sub"), None, None),
    )
    return jax.shard_map(
        per_device,
        mesh=mesh,
        in_specs=placed,
        out_specs=(
            P(("grp", "pool"), ("head", "sub"), None),
            P(("grp", "pool"), ("head", "sub"), None),
        ),
        check_vma=False,
    )
```

```python
import functools

import jax
import jax.numpy as jnp
import numpy as np
from jax import lax
from jax.experimental import pallas as pl
from jax.experimental.pallas import tpu as pltpu
from jax.sharding import PartitionSpec as P

EPS = 1e-06
SCALE = 192.0 ** (-0.5)
NONE = -1e30
BF = jnp.bfloat16
F32 = jnp.float32
LANES = 128
META = 32
NEW, TAIL_LEN, DEST, DEST_SLOT, COUNT = 0, 5, 6, 7, 8
LOG2E = 1.4426950408889634
ABSORB_UNROLL, SOFTEN_UNROLL, PROJECT_UNROLL = 32, 16, 32


def lane_ids(shape):
    return lax.broadcasted_iota(jnp.int32, shape, len(shape) - 1)


def row_ids(shape):
    return lax.broadcasted_iota(jnp.int32, shape, len(shape) - 2)


def rounded(values):
    return values.astype(BF).astype(F32)


def doubled(values):
    return jnp.concatenate([values, values], axis=-1)


def each_of(count, unroll, body):
    unroll = min(count, unroll)
    if unroll == count:
        for n in range(count):
            body(n)
    else:

        def some(n, carry):
            for m in range(unroll):
                body(n * unroll + m)
            return carry

        lax.fori_loop(0, count // unroll, some, 0)


def near_span(block, head_parts):
    span = block // head_parts
    return span if span % 16 == 0 else block


def copies_of(sources, targets, sems, pieces=1):
    copies = []
    for source, target in zip(sources, targets):
        size = source.shape[0] // pieces
        for n in range(pieces):
            part = pl.ds(n * size, size)
            copies.append(
                pltpu.make_async_copy(source.at[part], target.at[part], sems.at[len(copies)])
            )
    for copy in copies:
        copy.start()
    return copies


def load_kernel(head_parts, w_uk_hbm, pool_hbm, w_uk, keys, row_place, tail_place, pool, sems):
    copies = copies_of([pool_hbm, w_uk_hbm], [pool, w_uk], sems, 4)
    slots, block, width = pool.shape
    kvl = w_uk.shape[2]
    me = lax.axis_index("pool")

    owned = row_ids(row_place.shape) - me * slots
    row_place[...] = jnp.where(owned == lane_ids(row_place.shape) // block, 1.0, 0.0).astype(BF)
    span = near_span(block, head_parts)
    near = slots * span
    owned = row_ids(tail_place.shape) - me * slots
    lane = lane_ids(tail_place.shape)
    here = (owned == lane // span) & (lane < near)
    here = here | ((lane >= near) & (owned >= 0) & (owned < slots))
    tail_place[...] = jnp.where(here, 1.0, 0.0).astype(BF)

    for copy in copies[:4]:
        copy.wait()
    keys[:, :, 0:kvl] = pool[:, :, 0:kvl]
    keys[:, :, kvl:] = doubled(pool[:, :, kvl:])
    for copy in copies[4:]:
        copy.wait()


def query_kernel(wide, *refs):
    sources = refs[:8]
    message, home = refs[8:10]
    targets = refs[10:18]
    meta, sems = refs[18:]
    copies = copies_of(sources, targets, sems)
    for copy in copies:
        copy.wait()
    table, lengths, new_slot, q_nope, q_rope, new_latent, gain, freq = targets
    rows, heads, nope = q_nope.shape
    maxblk = table.shape[1]
    kvl = new_latent.shape[1] - q_rope.shape[2]
    queries = rows * heads
    whole = [q_nope[i].astype(F32) for i in range(rows)]

    lane = lane_ids((rows, LANES))
    row = row_ids((rows, LANES))
    position = jnp.full((rows, LANES), lengths[0], jnp.int32)
    for i in range(1, rows):
        position = jnp.where(row == i, lengths[i], position)
    angle = position.astype(F32) * freq[...]
    cosine = jnp.cos(angle)
    sine = jnp.sin(angle)
    sine = jnp.where(lane % 64 < 32, -sine, sine)
    qlane = lane_ids((heads, LANES))
    for i in range(rows):
        raw = doubled(q_rope[i].astype(F32))
        turned = raw * cosine[i : i + 1] + pltpu.roll(raw, 32, 1) * sine[i : i + 1]
        high = rounded(turned)
        whole.append(jnp.where(qlane < 64, high, turned - high))
    message[0 : 2 * queries, :] = jnp.concatenate(whole, axis=0).astype(BF)

    latent = new_latent[:, :kvl].astype(F32)
    square = jnp.mean(latent * latent, axis=-1, keepdims=True)
    gains = gain[...].astype(F32)
    gains = jnp.concatenate([gains[c : c + 1] for c in range(kvl // LANES)], axis=1)
    new_c = rounded(latent * lax.rsqrt(square + EPS) * gains)
    key = doubled(new_latent[:, kvl:].astype(F32))
    key = key * cosine + pltpu.roll(key, 32, 1) * sine
    home[...] = jnp.zeros_like(home)
    home[0:rows, 0:kvl] = new_c
    home[0:rows, kvl : kvl + LANES] = key
    meta[...] = jnp.zeros_like(meta)
    for c in range(kvl // LANES):
        meta[rows * (NEW + c) : rows * (NEW + c + 1), :] = new_c[:, c * LANES : (c + 1) * LANES]
    c = kvl // LANES
    meta[rows * (NEW + c) : rows * (NEW + c + 1), :] = key

    one = lane_ids((1, LANES))
    for i in range(rows):
        length = lengths[i]
        slot = new_slot[i]
        tail = table[i, length // 64]
        for n, value in ((TAIL_LEN, length % 64), (DEST, slot // rows), (DEST_SLOT, slot % rows)):
            at = rows * n + i
            meta[at : at + 1, :] = jnp.full((1, LANES), value, jnp.int32).astype(F32)
        counts = [jnp.zeros((1, LANES), jnp.int32) for _ in range(wide)]
        for j in range(maxblk):
            block = table[i, j]
            count = jnp.clip(length - 64 * j, 0, 64)
            for w in range(wide):
                counts[w] = counts[w] + jnp.where(one + w * LANES == block, count, 0)
        for w in range(wide):
            at = rows * (COUNT + w) + i
            meta[at : at + 1, :] = counts[w].astype(F32)
            at = rows * (COUNT + wide + w) + i
            meta[at : at + 1, :] = jnp.where(one + w * LANES == tail, 1.0, 0.0)
    message[2 * queries : 2 * queries + META, :] = meta[...].astype(BF)


def attend_kernel(owners, head_parts, rows, heads, *refs):
    messages = [refs[operand_orders(owners)[0].index(k)] for k in range(owners)]
    home, w_uk, pool, row_place, tail_place, w_uv_hbm = refs[owners : owners + 6]
    replies = refs[owners + 6 : 2 * owners + 6]
    w_uv, q_flat, lat, scores, weights, out, each, bias, tops, totals, new_scores, sems = refs[
        2 * owners + 6 :
    ]
    w_uv_copies = copies_of([w_uv_hbm], [w_uv], sems, 1)
    slots, block, width = pool.shape
    tokens = slots * block
    kvl = w_uk.shape[2]
    tiles = kvl // LANES
    queries = rows * heads
    everyone = owners * rows
    wide = (owners * slots + LANES - 1) // LANES
    me = lax.axis_index("pool")
    part = lax.axis_index(("head", "sub"))

    for k in range(owners):
        q_flat[k * queries : (k + 1) * queries, :] = messages[k][0:queries, :].astype(F32)
        told = messages[k][2 * queries : 2 * queries + META, :].astype(F32)
        for n in range(each.shape[0]):
            each[n, rows * k : rows * (k + 1), :] = told[rows * n : rows * (n + 1), :]

    def absorb(h):
        one_head = q_flat[pl.ds(h, everyone, stride=heads), :].astype(BF)
        absorbed = jnp.dot(one_head, w_uk[h], preferred_element_type=F32)
        for c in range(tiles):
            lat[c, pl.ds(h, everyone, stride=heads), :] = absorbed[:, c * LANES : (c + 1) * LANES]

    each_of(heads, ABSORB_UNROLL, absorb)

    counts = jnp.concatenate([each[COUNT + w] for w in range(wide)], axis=1).astype(BF)
    counts = jnp.dot(counts, row_place[...], preferred_element_type=F32)
    within = (lane_ids((everyone, tokens)) % block).astype(F32)
    bias[...] = jnp.where(within < counts, 0.0, NONE)

    turned = jnp.concatenate(
        [messages[k][queries : 2 * queries, :] for k in range(owners)], axis=0
    )
    flat_pool = pool[...].reshape(tokens, width)
    full = jnp.concatenate([lat[c].astype(BF) for c in range(tiles)] + [turned], axis=1)
    scores[...] = lax.dot_general(
        full, flat_pool, (((1,), (1,)), ((), ())), preferred_element_type=F32
    )

    span = block // head_parts
    tails = everyone * span
    reach = near_span(block, head_parts)
    near = slots * reach
    if reach == span:
        first = part * span
        near_pool = pool[:, pl.ds(pl.multiple_of(first, span), span), :].reshape(near, width)
    else:
        first = 0
        near_pool = flat_pool
    dest = (each[DEST].astype(jnp.int32) ^ me) * rows + each[DEST_SLOT].astype(jnp.int32)
    dest = jnp.concatenate([dest] * (tails // LANES), axis=1)
    goes = jnp.where(dest == lane_ids((everyone, tails)) // span, 1.0, 0.0).astype(BF)
    facts = [each[COUNT + wide + w] for w in range(wide)] + [each[TAIL_LEN]]
    facts = jnp.concatenate(facts + [each[NEW + c] for c in range(tiles + 1)], axis=1).astype(BF)
    facts = lax.dot_general(goes, facts, (((0,), (0,)), ((), ())), preferred_element_type=F32)
    is_last = facts[:, 0 : wide * LANES].astype(BF)
    tail_len = facts[:, wide * LANES : (wide + 1) * LANES]
    new_rows = facts[:, (wide + 1) * LANES :]
    chosen = jnp.dot(is_last, tail_place[...], preferred_element_type=F32)
    is_holder = chosen[:, near:] > 0.5
    token = (part * span + row_ids((tails, LANES)) % span).astype(F32)
    place = row_ids((tails, near))
    diagonal = part * span + place % span == first + lane_ids((tails, near)) % reach
    is_old = jnp.concatenate([token < tail_len] * (near // LANES), axis=1)
    chosen = jnp.where(diagonal & is_old, chosen[:, :near], 0.0).astype(BF)
    tail_rows = jnp.dot(chosen, near_pool, preferred_element_type=F32)
    is_new = is_holder & (token == tail_len)

    new_score = jnp.zeros((queries, LANES), F32)
    new_c = []
    for c in range(tiles):
        new_c.append(
            jnp.concatenate(
                [
                    jnp.broadcast_to(
                        home[r : r + 1, c * LANES : (c + 1) * LANES], (heads, LANES)
                    )
                    for r in range(rows)
                ],
                axis=0,
            )
        )
        new_score = new_score + rounded(lat[c, 0:queries, :]) * new_c[c]
    both = messages[0][queries : 2 * queries, :].astype(F32)
    both = both + pltpu.roll(both, 64, 1)
    new_key = jnp.concatenate(
        [
            jnp.broadcast_to(home[r : r + 1, kvl : kvl + LANES], (heads, LANES))
            for r in range(rows)
        ],
        axis=0,
    )
    new_score = new_score + 0.5 * both * new_key
    new_score = jnp.sum(new_score, axis=1, keepdims=True) * (SCALE * LOG2E)
    new_scores[...] = jnp.full(new_scores.shape, NONE, F32)
    new_scores[0:queries, :] = jnp.broadcast_to(new_score, (queries, LANES))

    chunk = 16

    def soften(n):
        at = pl.ds(pl.multiple_of(n * chunk, chunk), chunk)
        if heads >= chunk:
            shown = bias[pl.ds(n * chunk // heads, 1), :]
        else:
            shown = [bias[pl.ds(n * (chunk // heads) + m, 1), :] for m in range(chunk // heads)]
            shown = [jnp.broadcast_to(one, (heads, tokens)) for one in shown]
            shown = jnp.concatenate(shown, axis=0)
        some = scores[at, :] * (SCALE * LOG2E) + shown
        new = new_scores[at, 0:1]
        top = jnp.maximum(jnp.max(some, axis=1, keepdims=True), new)
        weight = jnp.exp2(some - top).astype(BF)
        weights[at, :] = weight
        total = jnp.sum(weight.astype(F32), axis=1, keepdims=True)
        total = jnp.where(top > 0.5 * NONE, total + rounded(jnp.exp2(new - top)), 0.0)
        tops[at, :] = jnp.broadcast_to(top, (chunk, LANES))
        totals[at, :] = jnp.broadcast_to(total, (chunk, LANES))

    each_of(owners * queries // chunk, SOFTEN_UNROLL, soften)
    sums = jnp.dot(weights[...], flat_pool[:, :kvl], preferred_element_type=F32)
    share = jnp.where(totals[...] > 0.0, 1.0 / jnp.maximum(totals[...], 1e-30), 0.0)
    new_weight = rounded(jnp.exp2(new_scores[0:queries, :] - tops[0:queries, :]))
    for c in range(tiles):
        some = sums[:, c * LANES : (c + 1) * LANES]
        lat[c, 0:queries, :] = (some[0:queries] + new_weight * new_c[c]) * share[0:queries]
        lat[c, queries:, :] = some[queries:] * share[queries:]

    for copy in w_uv_copies:
        copy.wait()

    def project(h):
        one_head = jnp.concatenate(
            [lat[c, pl.ds(h, everyone, stride=heads), :] for c in range(tiles)], axis=1
        ).astype(BF)
        out[pl.ds(h, everyone, stride=heads), :] = jnp.dot(
            one_head, w_uv[h], preferred_element_type=F32
        )

    each_of(heads, PROJECT_UNROLL, project)

    lane = lane_ids((heads, LANES))
    tail_lane = lane_ids((rows * span, LANES))
    for k in range(owners):
        mine = slice(k * rows * span, (k + 1) * rows * span)
        whole = [out[k * queries : (k + 1) * queries, :]]
        for c in range(tiles + 1):
            at = slice(c * LANES, (c + 1) * LANES)
            whole.append(tail_rows[mine, at] + jnp.where(is_new[mine], new_rows[mine, at], 0.0))
        stats = jnp.zeros((heads, LANES), F32)
        for i in range(rows):
            r = k * rows + i
            total = totals[r * heads : (r + 1) * heads, :]
            value = tops[r * heads : (r + 1) * heads, :] + jnp.log2(jnp.maximum(total, 1e-30))
            value = jnp.where(total > 0.0, value, NONE)
            for piece in range(3):
                high = rounded(value)
                stats = jnp.where(lane == 64 + 3 * i + piece, high, stats)
                value = value - high
        whole[-1] = jnp.where(tail_lane < 64, whole[-1], stats)
        whole = jnp.concatenate(whole, axis=0)
        missing = replies[k].shape[0] - whole.shape[0]
        if missing:
            whole = jnp.concatenate([whole, jnp.zeros((missing, LANES), F32)], axis=0)
        replies[k][...] = whole.astype(BF)


def combine_kernel(rows, heads, span, *refs):
    replies = [reply[...].astype(F32) for reply in refs[:-2]]
    attn_out, new_blocks = refs[-2:]
    kvl_tiles = new_blocks.shape[2] // LANES
    queries = rows * heads
    last = queries + kvl_tiles * rows * span
    stats = [reply[last : last + heads, :] for reply in replies]
    for i in range(rows):
        at = 64 + 3 * i
        sizes = [
            stat[:, at : at + 1] + stat[:, at + 1 : at + 2] + stat[:, at + 2 : at + 3]
            for stat in stats
        ]
        top = functools.reduce(jnp.maximum, sizes)
        shares = [jnp.exp2(size - top) for size in sizes]
        denominator = functools.reduce(jnp.add, shares)
        result = jnp.zeros((heads, LANES), F32)
        for share, reply in zip(shares, replies):
            result = result + share * reply[i * heads : (i + 1) * heads, :]
        attn_out[i] = (result / denominator).astype(BF)
    for c in range(kvl_tiles + 1):
        at = queries + c * rows * span
        tile = replies[0][at : at + rows * span, :]
        for reply in replies[1:]:
            tile = tile + reply[at : at + rows * span, :]
        left = min(LANES, new_blocks.shape[2] - c * LANES)
        for i in range(rows):
            new_blocks[i, :, c * LANES : c * LANES + left] = tile[
                i * span : (i + 1) * span, 0:left
            ].astype(BF)


def operand_orders(owners):
    if owners == 4:
        return (0, 1, 3, 2), (0, 3, 1, 2)
    return tuple(range(owners)), tuple(range(owners))


def per_device(
    pool, block_table, lengths, new_slot, q_nope, q_rope, new_latent, kv_gain, w_uk, w_uv
):
    owners = lax.axis_size("pool")
    parts = lax.axis_size(("head", "sub"))
    slots, block, width = pool.shape
    rows, heads, nope = q_nope.shape
    rope = q_rope.shape[2]
    kvl = kv_gain.shape[0]
    vdim = w_uv.shape[2]
    queries = rows * heads
    everyone = owners * rows
    wide = (owners * slots + LANES - 1) // LANES
    span = block // parts
    tokens = slots * block
    vmem = pl.BlockSpec(memory_space=pltpu.VMEM)
    hbm = pl.BlockSpec(memory_space=pltpu.HBM)

    half = rope // 2
    freq = 10000.0 ** (-(np.arange(LANES) % half).astype(np.float32) / np.float32(half))
    freq = jnp.asarray(freq.astype(np.float32)[None])
    gain = kv_gain.reshape(-1, LANES)
    raw = (block_table, lengths, new_slot, q_nope, q_rope, new_latent, gain, freq)
    raw = [pltpu.with_memory_space_constraint(a, pltpu.HBM) for a in raw]
    message, home = pl.pallas_call(
        functools.partial(query_kernel, wide),
        out_shape=(
            pltpu.VMEM((2 * queries + META, LANES), BF),
            pltpu.VMEM((8, kvl + LANES), F32),
        ),
        in_specs=[hbm] * len(raw),
        out_specs=(vmem, vmem),
        scratch_shapes=[
            (pltpu.SMEM if n < 3 else pltpu.VMEM)(a.shape, a.dtype) for n, a in enumerate(raw)
        ]
        + [pltpu.VMEM((META, LANES), F32), pltpu.SemaphoreType.DMA((len(raw),))],
        compiler_params=pltpu.CompilerParams(vmem_limit_bytes=4 * 2**20),
        name="queries",
    )(*raw)

    def swap(array, k):
        return lax.ppermute(array, "pool", [(i, i ^ k) for i in range(owners)])

    message_order, reply_order = operand_orders(owners)
    messages = [swap(message, k) if k else message for k in message_order]

    pool, w_uk, w_uv = [
        pltpu.with_memory_space_constraint(a, pltpu.HBM) for a in (pool, w_uk, w_uv)
    ]
    near = slots * near_span(block, parts)
    shapes = (w_uk.shape, pool.shape[:2] + (kvl + LANES,))
    shapes = shapes + ((wide * LANES, tokens), (wide * LANES, near + LANES))
    loaded = pl.pallas_call(
        functools.partial(load_kernel, parts),
        out_shape=tuple(pltpu.VMEM(shape, BF) for shape in shapes),
        in_specs=[hbm] * 2,
        out_specs=(vmem,) * 4,
        scratch_shapes=[pltpu.VMEM(pool.shape, BF), pltpu.SemaphoreType.DMA((8,))],
        compiler_params=pltpu.CompilerParams(vmem_limit_bytes=8 * 2**20),
        cost_estimate=pl.CostEstimate(flops=0, bytes_accessed=20 * 2**20, transcendentals=0),
        name="load",
    )(w_uk, pool)

    reply_rows = -(-(queries + (kvl // LANES + 1) * rows * span) // 16) * 16
    replies = pl.pallas_call(
        functools.partial(attend_kernel, owners, parts, rows, heads),
        out_shape=tuple(
            jax.ShapeDtypeStruct((reply_rows, LANES), BF) for _ in range(owners)
        ),
        in_specs=[vmem] * (owners + 5) + [hbm],
        out_specs=tuple([vmem] * owners),
        scratch_shapes=[
            pltpu.VMEM(w_uv.shape, BF),
            pltpu.VMEM((owners * queries, nope), F32),
            pltpu.VMEM((kvl // LANES, owners * queries, LANES), F32),
            pltpu.VMEM((owners * queries, tokens), F32),
            pltpu.VMEM((owners * queries, tokens), BF),
            pltpu.VMEM((owners * queries, vdim), F32),
            pltpu.VMEM((COUNT + 2 * wide, everyone, LANES), F32),
            pltpu.VMEM((everyone, tokens), F32),
            pltpu.VMEM((owners * queries, LANES), F32),
            pltpu.VMEM((owners * queries, LANES), F32),
            pltpu.VMEM((owners * queries, LANES), F32),
            pltpu.SemaphoreType.DMA((1,)),
        ],
        compiler_params=pltpu.CompilerParams(vmem_limit_bytes=24 * 2**20),
        name="attend",
    )(*messages, home, *loaded, w_uv)

    returned = [swap(replies[k], k) if k else replies[0] for k in reply_order]

    return pl.pallas_call(
        functools.partial(combine_kernel, rows, heads, span),
        out_shape=(
            jax.ShapeDtypeStruct((rows, heads, vdim), BF),
            jax.ShapeDtypeStruct((rows, span, width), BF),
        ),
        in_specs=[vmem] * owners,
        out_specs=(vmem, vmem),
        compiler_params=pltpu.CompilerParams(vmem_limit_bytes=4 * 2**20),
        name="combine",
    )(*returned)


def solution(mesh):
    placed = (
        P(("grp", "pool"), None, None),
        P(("grp", "pool"), None),
        P(("grp", "pool")),
        P(("grp", "pool")),
        P(("grp", "pool"), ("head", "sub"), None),
        P(("grp", "pool"), ("head", "sub"), None),
        P(("grp", "pool"), None),
        P(),
        P(("head", "sub"), None, None),
        P(("head", "sub"), None, None),
    )
    return jax.shard_map(
        per_device,
        mesh=mesh,
        in_specs=placed,
        out_specs=(
            P(("grp", "pool"), ("head", "sub"), None),
            P(("grp", "pool"), ("head", "sub"), None),
        ),
        check_vma=False,
    )
```

```python
import functools

import jax
import jax.numpy as jnp
import numpy as np
from jax import lax
from jax.experimental import pallas as pl
from jax.experimental.pallas import tpu as pltpu
from jax.sharding import PartitionSpec as P

EPS = 1e-06
SCALE = 192.0 ** (-0.5)
NONE = -1e30
BF = jnp.bfloat16
F32 = jnp.float32
LANES = 128
META = 32
NEW, TAIL_LEN, DEST, DEST_SLOT, COUNT = 0, 5, 6, 7, 8
LOG2E = 1.4426950408889634
ABSORB_UNROLL, SOFTEN_UNROLL, PROJECT_UNROLL = 32, 16, 32


def lane_ids(shape):
    return lax.broadcasted_iota(jnp.int32, shape, len(shape) - 1)


def row_ids(shape):
    return lax.broadcasted_iota(jnp.int32, shape, len(shape) - 2)


def rounded(values):
    return values.astype(BF).astype(F32)


def doubled(values):
    return jnp.concatenate([values, values], axis=-1)


def each_of(count, unroll, body):
    unroll = min(count, unroll)
    if unroll == count:
        for n in range(count):
            body(n)
    else:

        def some(n, carry):
            for m in range(unroll):
                body(n * unroll + m)
            return carry

        lax.fori_loop(0, count // unroll, some, 0)


def near_span(block, head_parts):
    span = block // head_parts
    return span if span % 16 == 0 else block


def copies_of(sources, targets, sems, pieces=1):
    copies = []
    for source, target in zip(sources, targets):
        size = source.shape[0] // pieces
        for n in range(pieces):
            part = pl.ds(n * size, size)
            copies.append(
                pltpu.make_async_copy(source.at[part], target.at[part], sems.at[len(copies)])
            )
    for copy in copies:
        copy.start()
    return copies


def load_kernel(head_parts, w_uk_hbm, pool_hbm, w_uk, keys, row_place, tail_place, pool, sems):
    copies = copies_of([pool_hbm, w_uk_hbm], [pool, w_uk], sems, 4)
    slots, block, width = pool.shape
    kvl = w_uk.shape[2]
    me = lax.axis_index("pool")

    owned = row_ids(row_place.shape) - me * slots
    row_place[...] = jnp.where(owned == lane_ids(row_place.shape) // block, 1.0, 0.0).astype(BF)
    span = near_span(block, head_parts)
    near = slots * span
    owned = row_ids(tail_place.shape) - me * slots
    lane = lane_ids(tail_place.shape)
    here = (owned == lane // span) & (lane < near)
    here = here | ((lane >= near) & (owned >= 0) & (owned < slots))
    tail_place[...] = jnp.where(here, 1.0, 0.0).astype(BF)

    for copy in copies[:4]:
        copy.wait()
    keys[:, :, 0:kvl] = pool[:, :, 0:kvl]
    keys[:, :, kvl:] = doubled(pool[:, :, kvl:])
    for copy in copies[4:]:
        copy.wait()


def query_kernel(wide, *refs):
    sources = refs[:8]
    message, home = refs[8:10]
    targets = refs[10:18]
    meta, sems = refs[18:]
    copies = copies_of(sources, targets, sems)
    for copy in copies:
        copy.wait()
    table, lengths, new_slot, q_nope, q_rope, new_latent, gain, freq = targets
    rows, heads, nope = q_nope.shape
    maxblk = table.shape[1]
    kvl = new_latent.shape[1] - q_rope.shape[2]
    queries = rows * heads
    whole = [q_nope[i].astype(F32) for i in range(rows)]

    lane = lane_ids((rows, LANES))
    row = row_ids((rows, LANES))
    position = jnp.full((rows, LANES), lengths[0], jnp.int32)
    for i in range(1, rows):
        position = jnp.where(row == i, lengths[i], position)
    angle = position.astype(F32) * freq[...]
    cosine = jnp.cos(angle)
    sine = jnp.sin(angle)
    sine = jnp.where(lane % 64 < 32, -sine, sine)
    qlane = lane_ids((heads, LANES))
    for i in range(rows):
        raw = doubled(q_rope[i].astype(F32))
        turned = raw * cosine[i : i + 1] + pltpu.roll(raw, 32, 1) * sine[i : i + 1]
        high = rounded(turned)
        whole.append(jnp.where(qlane < 64, high, turned - high))
    message[0 : 2 * queries, :] = jnp.concatenate(whole, axis=0).astype(BF)

    latent = new_latent[:, :kvl].astype(F32)
    square = jnp.mean(latent * latent, axis=-1, keepdims=True)
    gains = gain[...].astype(F32)
    gains = jnp.concatenate([gains[c : c + 1] for c in range(kvl // LANES)], axis=1)
    new_c = rounded(latent * lax.rsqrt(square + EPS) * gains)
    key = doubled(new_latent[:, kvl:].astype(F32))
    key = key * cosine + pltpu.roll(key, 32, 1) * sine
    home[...] = jnp.zeros_like(home)
    home[0:rows, 0:kvl] = new_c
    home[0:rows, kvl : kvl + LANES] = key
    meta[...] = jnp.zeros_like(meta)
    for c in range(kvl // LANES):
        meta[rows * (NEW + c) : rows * (NEW + c + 1), :] = new_c[:, c * LANES : (c + 1) * LANES]
    c = kvl // LANES
    meta[rows * (NEW + c) : rows * (NEW + c + 1), :] = key

    one = lane_ids((1, LANES))
    for i in range(rows):
        length = lengths[i]
        slot = new_slot[i]
        tail = table[i, length // 64]
        for n, value in ((TAIL_LEN, length % 64), (DEST, slot // rows), (DEST_SLOT, slot % rows)):
            at = rows * n + i
            meta[at : at + 1, :] = jnp.full((1, LANES), value, jnp.int32).astype(F32)
        counts = [jnp.zeros((1, LANES), jnp.int32) for _ in range(wide)]
        for j in range(maxblk):
            block = table[i, j]
            count = jnp.clip(length - 64 * j, 0, 64)
            for w in range(wide):
                counts[w] = counts[w] + jnp.where(one + w * LANES == block, count, 0)
        for w in range(wide):
            at = rows * (COUNT + w) + i
            meta[at : at + 1, :] = counts[w].astype(F32)
            at = rows * (COUNT + wide + w) + i
            meta[at : at + 1, :] = jnp.where(one + w * LANES == tail, 1.0, 0.0)
    message[2 * queries : 2 * queries + META, :] = meta[...].astype(BF)


def attend_kernel(owners, head_parts, rows, heads, *refs):
    messages = [refs[operand_orders(owners)[0].index(k)] for k in range(owners)]
    home, w_uk, pool, row_place, tail_place, w_uv_hbm = refs[owners : owners + 6]
    replies = refs[owners + 6 : 2 * owners + 6]
    w_uv, q_flat, lat, scores, weights, out, each, bias, tops, totals, new_scores, sems = refs[
        2 * owners + 6 :
    ]
    w_uv_copies = copies_of([w_uv_hbm], [w_uv], sems, 1)
    slots, block, width = pool.shape
    tokens = slots * block
    kvl = w_uk.shape[2]
    tiles = kvl // LANES
    queries = rows * heads
    everyone = owners * rows
    wide = (owners * slots + LANES - 1) // LANES
    me = lax.axis_index("pool")
    part = lax.axis_index(("head", "sub"))

    for k in range(owners):
        q_flat[k * queries : (k + 1) * queries, :] = messages[k][0:queries, :].astype(F32)
        told = messages[k][2 * queries : 2 * queries + META, :].astype(F32)
        for n in range(each.shape[0]):
            each[n, rows * k : rows * (k + 1), :] = told[rows * n : rows * (n + 1), :]

    none = jnp.zeros((everyone, LANES), F32)

    def absorb(pair):
        h = 2 * pair
        two = [q_flat[pl.ds(h + n, everyone, stride=heads), :] for n in range(2)]
        two = jnp.concatenate(
            [jnp.concatenate([two[0], none], axis=1), jnp.concatenate([none, two[1]], axis=1)],
            axis=0,
        ).astype(BF)
        absorbed = jnp.dot(
            two, w_uk[h : h + 2].reshape(2 * LANES, kvl), preferred_element_type=F32
        )
        for n in range(2):
            for c in range(tiles):
                lat[c, pl.ds(h + n, everyone, stride=heads), :] = absorbed[
                    n * everyone : (n + 1) * everyone, c * LANES : (c + 1) * LANES
                ]

    each_of(heads // 2, ABSORB_UNROLL, absorb)

    counts = jnp.concatenate([each[COUNT + w] for w in range(wide)], axis=1).astype(BF)
    counts = jnp.dot(counts, row_place[...], preferred_element_type=F32)
    within = (lane_ids((everyone, tokens)) % block).astype(F32)
    bias[...] = jnp.where(within < counts, 0.0, NONE)

    turned = jnp.concatenate(
        [messages[k][queries : 2 * queries, :] for k in range(owners)], axis=0
    )
    flat_pool = pool[...].reshape(tokens, width)
    full = jnp.concatenate([lat[c].astype(BF) for c in range(tiles)] + [turned], axis=1)
    scores[...] = lax.dot_general(
        full, flat_pool, (((1,), (1,)), ((), ())), preferred_element_type=F32
    )

    new_score = jnp.zeros((queries, LANES), F32)
    new_c = []
    for c in range(tiles):
        new_c.append(
            jnp.concatenate(
                [
                    jnp.broadcast_to(
                        home[r : r + 1, c * LANES : (c + 1) * LANES], (heads, LANES)
                    )
                    for r in range(rows)
                ],
                axis=0,
            )
        )
        new_score = new_score + rounded(lat[c, 0:queries, :]) * new_c[c]
    both = messages[0][queries : 2 * queries, :].astype(F32)
    both = both + pltpu.roll(both, 64, 1)
    new_key = jnp.concatenate(
        [
            jnp.broadcast_to(home[r : r + 1, kvl : kvl + LANES], (heads, LANES))
            for r in range(rows)
        ],
        axis=0,
    )
    new_score = new_score + 0.5 * both * new_key
    new_score = jnp.sum(new_score, axis=1, keepdims=True) * (SCALE * LOG2E)
    new_scores[...] = jnp.full(new_scores.shape, NONE, F32)
    new_scores[0:queries, :] = jnp.broadcast_to(new_score, (queries, LANES))

    chunk = 32

    def soften(n):
        at = pl.ds(pl.multiple_of(n * chunk, chunk), chunk)
        if heads >= chunk:
            shown = bias[pl.ds(n * chunk // heads, 1), :]
        else:
            shown = [bias[pl.ds(n * (chunk // heads) + m, 1), :] for m in range(chunk // heads)]
            shown = [jnp.broadcast_to(one, (heads, tokens)) for one in shown]
            shown = jnp.concatenate(shown, axis=0)
        some = scores[at, :] * (SCALE * LOG2E) + shown
        new = new_scores[at, 0:1]
        top = jnp.maximum(jnp.max(some, axis=1, keepdims=True), new)
        weight = jnp.exp2(some - top).astype(BF)
        weights[at, :] = weight
        total = jnp.sum(weight.astype(F32), axis=1, keepdims=True)
        total = jnp.where(top > 0.5 * NONE, total + rounded(jnp.exp2(new - top)), 0.0)
        tops[at, :] = jnp.broadcast_to(top, (chunk, LANES))
        totals[at, :] = jnp.broadcast_to(total, (chunk, LANES))

    each_of(owners * queries // chunk, SOFTEN_UNROLL, soften)
    span = block // head_parts
    tails = everyone * span
    reach = near_span(block, head_parts)
    near = slots * reach
    if reach == span:
        first = part * span
        near_pool = pool[:, pl.ds(pl.multiple_of(first, span), span), :].reshape(near, width)
    else:
        first = 0
        near_pool = flat_pool
    dest = (each[DEST].astype(jnp.int32) ^ me) * rows + each[DEST_SLOT].astype(jnp.int32)
    dest = jnp.concatenate([dest] * (tails // LANES), axis=1)
    goes = jnp.where(dest == lane_ids((everyone, tails)) // span, 1.0, 0.0).astype(BF)
    facts = [each[COUNT + wide + w] for w in range(wide)] + [each[TAIL_LEN]]
    facts = jnp.concatenate(facts + [each[NEW + c] for c in range(tiles + 1)], axis=1).astype(BF)
    facts = lax.dot_general(goes, facts, (((0,), (0,)), ((), ())), preferred_element_type=F32)
    is_last = facts[:, 0 : wide * LANES].astype(BF)
    tail_len = facts[:, wide * LANES : (wide + 1) * LANES]
    new_rows = facts[:, (wide + 1) * LANES :]
    chosen = jnp.dot(is_last, tail_place[...], preferred_element_type=F32)
    is_holder = chosen[:, near:] > 0.5
    token = (part * span + row_ids((tails, LANES)) % span).astype(F32)
    place = row_ids((tails, near))
    diagonal = part * span + place % span == first + lane_ids((tails, near)) % reach
    is_old = jnp.concatenate([token < tail_len] * (near // LANES), axis=1)
    chosen = jnp.where(diagonal & is_old, chosen[:, :near], 0.0).astype(BF)
    tail_rows = jnp.dot(chosen, near_pool, preferred_element_type=F32)
    is_new = is_holder & (token == tail_len)

    sums = jnp.dot(weights[...], flat_pool[:, :kvl], preferred_element_type=F32)
    share = jnp.where(totals[...] > 0.0, 1.0 / jnp.maximum(totals[...], 1e-30), 0.0)
    new_weight = rounded(jnp.exp2(new_scores[0:queries, :] - tops[0:queries, :]))
    for c in range(tiles):
        some = sums[:, c * LANES : (c + 1) * LANES]
        lat[c, 0:queries, :] = (some[0:queries] + new_weight * new_c[c]) * share[0:queries]
        lat[c, queries:, :] = some[queries:] * share[queries:]

    for copy in w_uv_copies:
        copy.wait()

    def project(h):
        two = jnp.concatenate(
            [
                jnp.concatenate(
                    [lat[c, pl.ds(2 * h + n, everyone, stride=heads), :] for c in range(tiles)], axis=1
                )
                for n in range(2)
            ],
            axis=0,
        ).astype(BF)
        both = jnp.dot(
            two, jnp.concatenate([w_uv[2 * h], w_uv[2 * h + 1]], axis=1), preferred_element_type=F32
        )
        for n in range(2):
            out[pl.ds(2 * h + n, everyone, stride=heads), :] = both[
                n * everyone : (n + 1) * everyone, n * LANES : (n + 1) * LANES
            ]

    each_of(heads // 2, PROJECT_UNROLL, project)

    lane = lane_ids((heads, LANES))
    tail_lane = lane_ids((rows * span, LANES))
    for k in range(owners):
        mine = slice(k * rows * span, (k + 1) * rows * span)
        whole = [out[k * queries : (k + 1) * queries, :]]
        for c in range(tiles + 1):
            at = slice(c * LANES, (c + 1) * LANES)
            whole.append(tail_rows[mine, at] + jnp.where(is_new[mine], new_rows[mine, at], 0.0))
        stats = jnp.zeros((heads, LANES), F32)
        for i in range(rows):
            r = k * rows + i
            total = totals[r * heads : (r + 1) * heads, :]
            value = tops[r * heads : (r + 1) * heads, :] + jnp.log2(jnp.maximum(total, 1e-30))
            value = jnp.where(total > 0.0, value, NONE)
            for piece in range(3):
                high = rounded(value)
                stats = jnp.where(lane == 64 + 3 * i + piece, high, stats)
                value = value - high
        whole[-1] = jnp.where(tail_lane < 64, whole[-1], stats)
        whole = jnp.concatenate(whole, axis=0)
        missing = replies[k].shape[0] - whole.shape[0]
        if missing:
            whole = jnp.concatenate([whole, jnp.zeros((missing, LANES), F32)], axis=0)
        replies[k][...] = whole.astype(BF)


def combine_kernel(rows, heads, span, *refs):
    replies = [reply[...].astype(F32) for reply in refs[:-2]]
    attn_out, new_blocks = refs[-2:]
    kvl_tiles = new_blocks.shape[2] // LANES
    queries = rows * heads
    last = queries + kvl_tiles * rows * span
    stats = [reply[last : last + heads, :] for reply in replies]
    for i in range(rows):
        at = 64 + 3 * i
        sizes = [
            stat[:, at : at + 1] + stat[:, at + 1 : at + 2] + stat[:, at + 2 : at + 3]
            for stat in stats
        ]
        top = functools.reduce(jnp.maximum, sizes)
        shares = [jnp.exp2(size - top) for size in sizes]
        denominator = functools.reduce(jnp.add, shares)
        result = jnp.zeros((heads, LANES), F32)
        for share, reply in zip(shares, replies):
            result = result + share * reply[i * heads : (i + 1) * heads, :]
        attn_out[i] = (result / denominator).astype(BF)
    for c in range(kvl_tiles + 1):
        at = queries + c * rows * span
        tile = replies[0][at : at + rows * span, :]
        for reply in replies[1:]:
            tile = tile + reply[at : at + rows * span, :]
        left = min(LANES, new_blocks.shape[2] - c * LANES)
        for i in range(rows):
            new_blocks[i, :, c * LANES : c * LANES + left] = tile[
                i * span : (i + 1) * span, 0:left
            ].astype(BF)


def operand_orders(owners):
    if owners == 4:
        return (0, 1, 3, 2), (0, 3, 1, 2)
    return tuple(range(owners)), tuple(range(owners))


def per_device(
    pool, block_table, lengths, new_slot, q_nope, q_rope, new_latent, kv_gain, w_uk, w_uv
):
    owners = lax.axis_size("pool")
    parts = lax.axis_size(("head", "sub"))
    slots, block, width = pool.shape
    rows, heads, nope = q_nope.shape
    rope = q_rope.shape[2]
    kvl = kv_gain.shape[0]
    vdim = w_uv.shape[2]
    queries = rows * heads
    everyone = owners * rows
    wide = (owners * slots + LANES - 1) // LANES
    span = block // parts
    tokens = slots * block
    vmem = pl.BlockSpec(memory_space=pltpu.VMEM)
    hbm = pl.BlockSpec(memory_space=pltpu.HBM)

    half = rope // 2
    freq = 10000.0 ** (-(np.arange(LANES) % half).astype(np.float32) / np.float32(half))
    freq = jnp.asarray(freq.astype(np.float32)[None])
    gain = kv_gain.reshape(-1, LANES)
    raw = (block_table, lengths, new_slot, q_nope, q_rope, new_latent, gain, freq)
    raw = [pltpu.with_memory_space_constraint(a, pltpu.HBM) for a in raw]
    message, home = pl.pallas_call(
        functools.partial(query_kernel, wide),
        out_shape=(
            pltpu.VMEM((2 * queries + META, LANES), BF),
            pltpu.VMEM((8, kvl + LANES), F32),
        ),
        in_specs=[hbm] * len(raw),
        out_specs=(vmem, vmem),
        scratch_shapes=[
            (pltpu.SMEM if n < 3 else pltpu.VMEM)(a.shape, a.dtype) for n, a in enumerate(raw)
        ]
        + [pltpu.VMEM((META, LANES), F32), pltpu.SemaphoreType.DMA((len(raw),))],
        compiler_params=pltpu.CompilerParams(vmem_limit_bytes=4 * 2**20),
        name="queries",
    )(*raw)

    def swap(array, k):
        return lax.ppermute(array, "pool", [(i, i ^ k) for i in range(owners)])

    message_order, reply_order = operand_orders(owners)
    messages = [swap(message, k) if k else message for k in message_order]

    pool, w_uk, w_uv = [
        pltpu.with_memory_space_constraint(a, pltpu.HBM) for a in (pool, w_uk, w_uv)
    ]
    near = slots * near_span(block, parts)
    shapes = (w_uk.shape, pool.shape[:2] + (kvl + LANES,))
    shapes = shapes + ((wide * LANES, tokens), (wide * LANES, near + LANES))
    loaded = pl.pallas_call(
        functools.partial(load_kernel, parts),
        out_shape=tuple(pltpu.VMEM(shape, BF) for shape in shapes),
        in_specs=[hbm] * 2,
        out_specs=(vmem,) * 4,
        scratch_shapes=[pltpu.VMEM(pool.shape, BF), pltpu.SemaphoreType.DMA((8,))],
        compiler_params=pltpu.CompilerParams(vmem_limit_bytes=8 * 2**20),
        cost_estimate=pl.CostEstimate(flops=0, bytes_accessed=20 * 2**20, transcendentals=0),
        name="load",
    )(w_uk, pool)

    reply_rows = -(-(queries + (kvl // LANES + 1) * rows * span) // 16) * 16
    replies = pl.pallas_call(
        functools.partial(attend_kernel, owners, parts, rows, heads),
        out_shape=tuple(
            jax.ShapeDtypeStruct((reply_rows, LANES), BF) for _ in range(owners)
        ),
        in_specs=[vmem] * (owners + 5) + [hbm],
        out_specs=tuple([vmem] * owners),
        scratch_shapes=[
            pltpu.VMEM(w_uv.shape, BF),
            pltpu.VMEM((owners * queries, nope), F32),
            pltpu.VMEM((kvl // LANES, owners * queries, LANES), F32),
            pltpu.VMEM((owners * queries, tokens), F32),
            pltpu.VMEM((owners * queries, tokens), BF),
            pltpu.VMEM((owners * queries, vdim), F32),
            pltpu.VMEM((COUNT + 2 * wide, everyone, LANES), F32),
            pltpu.VMEM((everyone, tokens), F32),
            pltpu.VMEM((owners * queries, LANES), F32),
            pltpu.VMEM((owners * queries, LANES), F32),
            pltpu.VMEM((owners * queries, LANES), F32),
            pltpu.SemaphoreType.DMA((1,)),
        ],
        compiler_params=pltpu.CompilerParams(vmem_limit_bytes=24 * 2**20),
        name="attend",
    )(*messages, home, *loaded, w_uv)

    returned = [swap(replies[k], k) if k else replies[0] for k in reply_order]

    return pl.pallas_call(
        functools.partial(combine_kernel, rows, heads, span),
        out_shape=(
            jax.ShapeDtypeStruct((rows, heads, vdim), BF),
            jax.ShapeDtypeStruct((rows, span, width), BF),
        ),
        in_specs=[vmem] * owners,
        out_specs=(vmem, vmem),
        compiler_params=pltpu.CompilerParams(vmem_limit_bytes=4 * 2**20),
        name="combine",
    )(*returned)


def solution(mesh):
    placed = (
        P(("grp", "pool"), None, None),
        P(("grp", "pool"), None),
        P(("grp", "pool")),
        P(("grp", "pool")),
        P(("grp", "pool"), ("head", "sub"), None),
        P(("grp", "pool"), ("head", "sub"), None),
        P(("grp", "pool"), None),
        P(),
        P(("head", "sub"), None, None),
        P(("head", "sub"), None, None),
    )
    return jax.shard_map(
        per_device,
        mesh=mesh,
        in_specs=placed,
        out_specs=(
            P(("grp", "pool"), ("head", "sub"), None),
            P(("grp", "pool"), ("head", "sub"), None),
        ),
        check_vma=False,
    )
```

```python
import functools

import jax
import jax.numpy as jnp
import numpy as np
from jax import lax
from jax.experimental import pallas as pl
from jax.experimental.pallas import tpu as pltpu
from jax.sharding import PartitionSpec as P

EPS = 1e-06
SCALE = 192.0 ** (-0.5)
NONE = -1e30
BF = jnp.bfloat16
F32 = jnp.float32
LANES = 128
META = 32
NEW, TAIL_LEN, DEST, DEST_SLOT, COUNT = 0, 5, 6, 7, 8
LOG2E = 1.4426950408889634
ABSORB_UNROLL, SOFTEN_UNROLL, PROJECT_UNROLL = 32, 16, 32


def lane_ids(shape):
    return lax.broadcasted_iota(jnp.int32, shape, len(shape) - 1)


def row_ids(shape):
    return lax.broadcasted_iota(jnp.int32, shape, len(shape) - 2)


def rounded(values):
    return values.astype(BF).astype(F32)


def doubled(values):
    return jnp.concatenate([values, values], axis=-1)


def each_of(count, unroll, body):
    unroll = min(count, unroll)
    if unroll == count:
        for n in range(count):
            body(n)
    else:

        def some(n, carry):
            for m in range(unroll):
                body(n * unroll + m)
            return carry

        lax.fori_loop(0, count // unroll, some, 0)


def near_span(block, head_parts):
    span = block // head_parts
    return span if span % 16 == 0 else block


def copies_of(sources, targets, sems, pieces=1):
    copies = []
    for source, target in zip(sources, targets):
        size = source.shape[0] // pieces
        for n in range(pieces):
            part = pl.ds(n * size, size)
            copies.append(
                pltpu.make_async_copy(source.at[part], target.at[part], sems.at[len(copies)])
            )
    for copy in copies:
        copy.start()
    return copies


def load_kernel(head_parts, w_uk_hbm, pool_hbm, w_uk, keys, row_place, tail_place, pool, sems):
    copies = copies_of([pool_hbm, w_uk_hbm], [pool, w_uk], sems, 4)
    slots, block, width = pool.shape
    kvl = w_uk.shape[2]
    me = lax.axis_index("pool")

    owned = row_ids(row_place.shape) - me * slots
    row_place[...] = jnp.where(owned == lane_ids(row_place.shape) // block, 1.0, 0.0).astype(BF)
    span = near_span(block, head_parts)
    near = slots * span
    owned = row_ids(tail_place.shape) - me * slots
    lane = lane_ids(tail_place.shape)
    here = (owned == lane // span) & (lane < near)
    here = here | ((lane >= near) & (owned >= 0) & (owned < slots))
    tail_place[...] = jnp.where(here, 1.0, 0.0).astype(BF)

    for copy in copies[:4]:
        copy.wait()
    keys[:, :, 0:kvl] = pool[:, :, 0:kvl]
    keys[:, :, kvl:] = doubled(pool[:, :, kvl:])
    for copy in copies[4:]:
        copy.wait()


def query_kernel(wide, *refs):
    sources = refs[:8]
    message, home = refs[8:10]
    targets = refs[10:18]
    meta, sems = refs[18:]
    copies = copies_of(sources, targets, sems)
    for copy in copies:
        copy.wait()
    table, lengths, new_slot, q_nope, q_rope, new_latent, gain, freq = targets
    rows, heads, nope = q_nope.shape
    maxblk = table.shape[1]
    kvl = new_latent.shape[1] - q_rope.shape[2]
    queries = rows * heads
    whole = [q_nope[i].astype(F32) for i in range(rows)]

    lane = lane_ids((rows, LANES))
    row = row_ids((rows, LANES))
    position = jnp.full((rows, LANES), lengths[0], jnp.int32)
    for i in range(1, rows):
        position = jnp.where(row == i, lengths[i], position)
    angle = position.astype(F32) * freq[...]
    cosine = jnp.cos(angle)
    sine = jnp.sin(angle)
    sine = jnp.where(lane % 64 < 32, -sine, sine)
    qlane = lane_ids((heads, LANES))
    for i in range(rows):
        raw = doubled(q_rope[i].astype(F32))
        turned = raw * cosine[i : i + 1] + pltpu.roll(raw, 32, 1) * sine[i : i + 1]
        high = rounded(turned)
        whole.append(jnp.where(qlane < 64, high, turned - high))
    message[0 : 2 * queries, :] = jnp.concatenate(whole, axis=0).astype(BF)

    latent = new_latent[:, :kvl].astype(F32)
    square = jnp.mean(latent * latent, axis=-1, keepdims=True)
    gains = gain[...].astype(F32)
    gains = jnp.concatenate([gains[c : c + 1] for c in range(kvl // LANES)], axis=1)
    new_c = rounded(latent * lax.rsqrt(square + EPS) * gains)
    key = doubled(new_latent[:, kvl:].astype(F32))
    key = key * cosine + pltpu.roll(key, 32, 1) * sine
    home[...] = jnp.zeros_like(home)
    home[0:rows, 0:kvl] = new_c
    home[0:rows, kvl : kvl + LANES] = key
    meta[...] = jnp.zeros_like(meta)
    for c in range(kvl // LANES):
        meta[rows * (NEW + c) : rows * (NEW + c + 1), :] = new_c[:, c * LANES : (c + 1) * LANES]
    c = kvl // LANES
    meta[rows * (NEW + c) : rows * (NEW + c + 1), :] = key

    one = lane_ids((1, LANES))
    for i in range(rows):
        length = lengths[i]
        slot = new_slot[i]
        tail = table[i, length // 64]
        for n, value in ((TAIL_LEN, length % 64), (DEST, slot // rows), (DEST_SLOT, slot % rows)):
            at = rows * n + i
            meta[at : at + 1, :] = jnp.full((1, LANES), value, jnp.int32).astype(F32)
        counts = [jnp.zeros((1, LANES), jnp.int32) for _ in range(wide)]
        for j in range(maxblk):
            block = table[i, j]
            count = jnp.clip(length - 64 * j, 0, 64)
            for w in range(wide):
                counts[w] = counts[w] + jnp.where(one + w * LANES == block, count, 0)
        for w in range(wide):
            at = rows * (COUNT + w) + i
            meta[at : at + 1, :] = counts[w].astype(F32)
            at = rows * (COUNT + wide + w) + i
            meta[at : at + 1, :] = jnp.where(one + w * LANES == tail, 1.0, 0.0)
    message[2 * queries : 2 * queries + META, :] = meta[...].astype(BF)


def attend_kernel(owners, head_parts, rows, heads, *refs):
    messages = [refs[operand_orders(owners)[0].index(k)] for k in range(owners)]
    home, w_uk, pool, row_place, tail_place, w_uv_hbm = refs[owners : owners + 6]
    replies = refs[owners + 6 : 2 * owners + 6]
    w_uv, q_flat, lat, scores, weights, out, each, bias, tops, totals, new_scores, sems = refs[
        2 * owners + 6 :
    ]
    w_uv_copies = copies_of([w_uv_hbm], [w_uv], sems, 1)
    slots, block, width = pool.shape
    tokens = slots * block
    kvl = w_uk.shape[2]
    tiles = kvl // LANES
    queries = rows * heads
    everyone = owners * rows
    wide = (owners * slots + LANES - 1) // LANES
    me = lax.axis_index("pool")
    part = lax.axis_index(("head", "sub"))

    for k in range(owners):
        q_flat[k * queries : (k + 1) * queries, :] = messages[k][0:queries, :].astype(F32)
        told = messages[k][2 * queries : 2 * queries + META, :].astype(F32)
        for n in range(each.shape[0]):
            each[n, rows * k : rows * (k + 1), :] = told[rows * n : rows * (n + 1), :]

    none = jnp.zeros((everyone, LANES), F32)

    def absorb(pair):
        h = 2 * pair
        two = [q_flat[pl.ds(h + n, everyone, stride=heads), :] for n in range(2)]
        two = jnp.concatenate(
            [jnp.concatenate([two[0], none], axis=1), jnp.concatenate([none, two[1]], axis=1)],
            axis=0,
        ).astype(BF)
        absorbed = jnp.dot(
            two, w_uk[h : h + 2].reshape(2 * LANES, kvl), preferred_element_type=F32
        )
        for n in range(2):
            for c in range(tiles):
                lat[c, pl.ds(h + n, everyone, stride=heads), :] = absorbed[
                    n * everyone : (n + 1) * everyone, c * LANES : (c + 1) * LANES
                ]

    each_of(heads // 2, ABSORB_UNROLL, absorb)

    counts = jnp.concatenate([each[COUNT + w] for w in range(wide)], axis=1).astype(BF)
    counts = jnp.dot(counts, row_place[...], preferred_element_type=F32)
    within = (lane_ids((everyone, tokens)) % block).astype(F32)
    bias[...] = jnp.where(within < counts, 0.0, NONE)

    turned = jnp.concatenate(
        [messages[k][queries : 2 * queries, :] for k in range(owners)], axis=0
    )
    flat_pool = pool[...].reshape(tokens, width)
    full = jnp.concatenate([lat[c].astype(BF) for c in range(tiles)] + [turned], axis=1)
    scores[...] = lax.dot_general(
        full, flat_pool, (((1,), (1,)), ((), ())), preferred_element_type=F32
    )

    new_score = jnp.zeros((queries, LANES), F32)
    new_c = []
    for c in range(tiles):
        new_c.append(
            jnp.concatenate(
                [
                    jnp.broadcast_to(
                        home[r : r + 1, c * LANES : (c + 1) * LANES], (heads, LANES)
                    )
                    for r in range(rows)
                ],
                axis=0,
            )
        )
        new_score = new_score + rounded(lat[c, 0:queries, :]) * new_c[c]
    both = messages[0][queries : 2 * queries, :].astype(F32)
    both = both + pltpu.roll(both, 64, 1)
    new_key = jnp.concatenate(
        [
            jnp.broadcast_to(home[r : r + 1, kvl : kvl + LANES], (heads, LANES))
            for r in range(rows)
        ],
        axis=0,
    )
    new_score = new_score + 0.5 * both * new_key
    new_score = jnp.sum(new_score, axis=1, keepdims=True) * (SCALE * LOG2E)
    new_scores[...] = jnp.full(new_scores.shape, NONE, F32)
    new_scores[0:queries, :] = jnp.broadcast_to(new_score, (queries, LANES))

    chunk = 32

    def soften(n):
        at = pl.ds(pl.multiple_of(n * chunk, chunk), chunk)
        if heads >= chunk:
            shown = bias[pl.ds(n * chunk // heads, 1), :]
        else:
            shown = [bias[pl.ds(n * (chunk // heads) + m, 1), :] for m in range(chunk // heads)]
            shown = [jnp.broadcast_to(one, (heads, tokens)) for one in shown]
            shown = jnp.concatenate(shown, axis=0)
        some = scores[at, :] * (SCALE * LOG2E) + shown
        new = new_scores[at, 0:1]
        top = jnp.maximum(jnp.max(some, axis=1, keepdims=True), new)
        weight = jnp.exp2(some - top)
        weights[at, :] = weight.astype(BF)
        total = jnp.sum(weight, axis=1, keepdims=True)
        total = jnp.where(top > 0.5 * NONE, total + rounded(jnp.exp2(new - top)), 0.0)
        tops[at, :] = jnp.broadcast_to(top, (chunk, LANES))
        totals[at, :] = jnp.broadcast_to(total, (chunk, LANES))

    each_of(owners * queries // chunk, SOFTEN_UNROLL, soften)
    span = block // head_parts
    tails = everyone * span
    reach = near_span(block, head_parts)
    near = slots * reach
    if reach == span:
        first = part * span
        near_pool = pool[:, pl.ds(pl.multiple_of(first, span), span), :].reshape(near, width)
    else:
        first = 0
        near_pool = flat_pool
    dest = (each[DEST].astype(jnp.int32) ^ me) * rows + each[DEST_SLOT].astype(jnp.int32)
    dest = jnp.concatenate([dest] * (tails // LANES), axis=1)
    goes = jnp.where(dest == lane_ids((everyone, tails)) // span, 1.0, 0.0).astype(BF)
    facts = [each[COUNT + wide + w] for w in range(wide)] + [each[TAIL_LEN]]
    facts = jnp.concatenate(facts + [each[NEW + c] for c in range(tiles + 1)], axis=1).astype(BF)
    facts = lax.dot_general(goes, facts, (((0,), (0,)), ((), ())), preferred_element_type=F32)
    is_last = facts[:, 0 : wide * LANES].astype(BF)
    tail_len = facts[:, wide * LANES : (wide + 1) * LANES]
    new_rows = facts[:, (wide + 1) * LANES :]
    chosen = jnp.dot(is_last, tail_place[...], preferred_element_type=F32)
    is_holder = chosen[:, near:] > 0.5
    token = (part * span + row_ids((tails, LANES)) % span).astype(F32)
    place = row_ids((tails, near))
    diagonal = part * span + place % span == first + lane_ids((tails, near)) % reach
    is_old = jnp.concatenate([token < tail_len] * (near // LANES), axis=1)
    chosen = jnp.where(diagonal & is_old, chosen[:, :near], 0.0).astype(BF)
    tail_rows = jnp.dot(chosen, near_pool, preferred_element_type=F32)
    is_new = is_holder & (token == tail_len)

    sums = jnp.dot(weights[...], flat_pool[:, :kvl], preferred_element_type=F32)
    share = jnp.where(totals[...] > 0.0, 1.0 / jnp.maximum(totals[...], 1e-30), 0.0)
    new_weight = rounded(jnp.exp2(new_scores[0:queries, :] - tops[0:queries, :]))
    for c in range(tiles):
        some = sums[:, c * LANES : (c + 1) * LANES]
        lat[c, 0:queries, :] = (some[0:queries] + new_weight * new_c[c]) * share[0:queries]
        lat[c, queries:, :] = some[queries:] * share[queries:]

    for copy in w_uv_copies:
        copy.wait()

    def project(h):
        two = jnp.concatenate(
            [
                jnp.concatenate(
                    [lat[c, pl.ds(2 * h + n, everyone, stride=heads), :] for c in range(tiles)], axis=1
                )
                for n in range(2)
            ],
            axis=0,
        ).astype(BF)
        both = jnp.dot(
            two, jnp.concatenate([w_uv[2 * h], w_uv[2 * h + 1]], axis=1), preferred_element_type=F32
        )
        for n in range(2):
            out[pl.ds(2 * h + n, everyone, stride=heads), :] = both[
                n * everyone : (n + 1) * everyone, n * LANES : (n + 1) * LANES
            ]

    each_of(heads // 2, PROJECT_UNROLL, project)

    lane = lane_ids((heads, LANES))
    tail_lane = lane_ids((rows * span, LANES))
    for k in range(owners):
        mine = slice(k * rows * span, (k + 1) * rows * span)
        whole = [out[k * queries : (k + 1) * queries, :]]
        for c in range(tiles + 1):
            at = slice(c * LANES, (c + 1) * LANES)
            whole.append(tail_rows[mine, at] + jnp.where(is_new[mine], new_rows[mine, at], 0.0))
        stats = jnp.zeros((heads, LANES), F32)
        for i in range(rows):
            r = k * rows + i
            total = totals[r * heads : (r + 1) * heads, :]
            value = tops[r * heads : (r + 1) * heads, :] + jnp.log2(jnp.maximum(total, 1e-30))
            value = jnp.where(total > 0.0, value, NONE)
            for piece in range(3):
                high = rounded(value)
                stats = jnp.where(lane == 64 + 3 * i + piece, high, stats)
                value = value - high
        whole[-1] = jnp.where(tail_lane < 64, whole[-1], stats)
        whole = jnp.concatenate(whole, axis=0)
        missing = replies[k].shape[0] - whole.shape[0]
        if missing:
            whole = jnp.concatenate([whole, jnp.zeros((missing, LANES), F32)], axis=0)
        replies[k][...] = whole.astype(BF)


def combine_kernel(rows, heads, span, *refs):
    replies = [reply[...].astype(F32) for reply in refs[:-2]]
    attn_out, new_blocks = refs[-2:]
    kvl_tiles = new_blocks.shape[2] // LANES
    queries = rows * heads
    last = queries + kvl_tiles * rows * span
    stats = [reply[last : last + heads, :] for reply in replies]
    for i in range(rows):
        at = 64 + 3 * i
        sizes = [
            stat[:, at : at + 1] + stat[:, at + 1 : at + 2] + stat[:, at + 2 : at + 3]
            for stat in stats
        ]
        top = functools.reduce(jnp.maximum, sizes)
        shares = [jnp.exp2(size - top) for size in sizes]
        denominator = functools.reduce(jnp.add, shares)
        result = jnp.zeros((heads, LANES), F32)
        for share, reply in zip(shares, replies):
            result = result + share * reply[i * heads : (i + 1) * heads, :]
        attn_out[i] = (result / denominator).astype(BF)
    for c in range(kvl_tiles + 1):
        at = queries + c * rows * span
        tile = replies[0][at : at + rows * span, :]
        for reply in replies[1:]:
            tile = tile + reply[at : at + rows * span, :]
        left = min(LANES, new_blocks.shape[2] - c * LANES)
        for i in range(rows):
            new_blocks[i, :, c * LANES : c * LANES + left] = tile[
                i * span : (i + 1) * span, 0:left
            ].astype(BF)


def operand_orders(owners):
    if owners == 4:
        return (0, 1, 3, 2), (0, 3, 1, 2)
    return tuple(range(owners)), tuple(range(owners))


def per_device(
    pool, block_table, lengths, new_slot, q_nope, q_rope, new_latent, kv_gain, w_uk, w_uv
):
    owners = lax.axis_size("pool")
    parts = lax.axis_size(("head", "sub"))
    slots, block, width = pool.shape
    rows, heads, nope = q_nope.shape
    rope = q_rope.shape[2]
    kvl = kv_gain.shape[0]
    vdim = w_uv.shape[2]
    queries = rows * heads
    everyone = owners * rows
    wide = (owners * slots + LANES - 1) // LANES
    span = block // parts
    tokens = slots * block
    vmem = pl.BlockSpec(memory_space=pltpu.VMEM)
    hbm = pl.BlockSpec(memory_space=pltpu.HBM)

    half = rope // 2
    freq = 10000.0 ** (-(np.arange(LANES) % half).astype(np.float32) / np.float32(half))
    freq = jnp.asarray(freq.astype(np.float32)[None])
    gain = kv_gain.reshape(-1, LANES)
    raw = (block_table, lengths, new_slot, q_nope, q_rope, new_latent, gain, freq)
    raw = [pltpu.with_memory_space_constraint(a, pltpu.HBM) for a in raw]
    message, home = pl.pallas_call(
        functools.partial(query_kernel, wide),
        out_shape=(
            pltpu.VMEM((2 * queries + META, LANES), BF),
            pltpu.VMEM((8, kvl + LANES), F32),
        ),
        in_specs=[hbm] * len(raw),
        out_specs=(vmem, vmem),
        scratch_shapes=[
            (pltpu.SMEM if n < 3 else pltpu.VMEM)(a.shape, a.dtype) for n, a in enumerate(raw)
        ]
        + [pltpu.VMEM((META, LANES), F32), pltpu.SemaphoreType.DMA((len(raw),))],
        compiler_params=pltpu.CompilerParams(vmem_limit_bytes=4 * 2**20),
        name="queries",
    )(*raw)

    def swap(array, k):
        return lax.ppermute(array, "pool", [(i, i ^ k) for i in range(owners)])

    message_order, reply_order = operand_orders(owners)
    messages = [swap(message, k) if k else message for k in message_order]

    pool, w_uk, w_uv = [
        pltpu.with_memory_space_constraint(a, pltpu.HBM) for a in (pool, w_uk, w_uv)
    ]
    near = slots * near_span(block, parts)
    shapes = (w_uk.shape, pool.shape[:2] + (kvl + LANES,))
    shapes = shapes + ((wide * LANES, tokens), (wide * LANES, near + LANES))
    loaded = pl.pallas_call(
        functools.partial(load_kernel, parts),
        out_shape=tuple(pltpu.VMEM(shape, BF) for shape in shapes),
        in_specs=[hbm] * 2,
        out_specs=(vmem,) * 4,
        scratch_shapes=[pltpu.VMEM(pool.shape, BF), pltpu.SemaphoreType.DMA((8,))],
        compiler_params=pltpu.CompilerParams(vmem_limit_bytes=8 * 2**20),
        cost_estimate=pl.CostEstimate(flops=0, bytes_accessed=20 * 2**20, transcendentals=0),
        name="load",
    )(w_uk, pool)

    reply_rows = -(-(queries + (kvl // LANES + 1) * rows * span) // 16) * 16
    replies = pl.pallas_call(
        functools.partial(attend_kernel, owners, parts, rows, heads),
        out_shape=tuple(
            jax.ShapeDtypeStruct((reply_rows, LANES), BF) for _ in range(owners)
        ),
        in_specs=[vmem] * (owners + 5) + [hbm],
        out_specs=tuple([vmem] * owners),
        scratch_shapes=[
            pltpu.VMEM(w_uv.shape, BF),
            pltpu.VMEM((owners * queries, nope), F32),
            pltpu.VMEM((kvl // LANES, owners * queries, LANES), F32),
            pltpu.VMEM((owners * queries, tokens), F32),
            pltpu.VMEM((owners * queries, tokens), BF),
            pltpu.VMEM((owners * queries, vdim), F32),
            pltpu.VMEM((COUNT + 2 * wide, everyone, LANES), F32),
            pltpu.VMEM((everyone, tokens), F32),
            pltpu.VMEM((owners * queries, LANES), F32),
            pltpu.VMEM((owners * queries, LANES), F32),
            pltpu.VMEM((owners * queries, LANES), F32),
            pltpu.SemaphoreType.DMA((1,)),
        ],
        compiler_params=pltpu.CompilerParams(vmem_limit_bytes=24 * 2**20),
        name="attend",
    )(*messages, home, *loaded, w_uv)

    returned = [swap(replies[k], k) if k else replies[0] for k in reply_order]

    return pl.pallas_call(
        functools.partial(combine_kernel, rows, heads, span),
        out_shape=(
            jax.ShapeDtypeStruct((rows, heads, vdim), BF),
            jax.ShapeDtypeStruct((rows, span, width), BF),
        ),
        in_specs=[vmem] * owners,
        out_specs=(vmem, vmem),
        compiler_params=pltpu.CompilerParams(vmem_limit_bytes=4 * 2**20),
        name="combine",
    )(*returned)


def solution(mesh):
    placed = (
        P(("grp", "pool"), None, None),
        P(("grp", "pool"), None),
        P(("grp", "pool")),
        P(("grp", "pool")),
        P(("grp", "pool"), ("head", "sub"), None),
        P(("grp", "pool"), ("head", "sub"), None),
        P(("grp", "pool"), None),
        P(),
        P(("head", "sub"), None, None),
        P(("head", "sub"), None, None),
    )
    return jax.shard_map(
        per_device,
        mesh=mesh,
        in_specs=placed,
        out_specs=(
            P(("grp", "pool"), ("head", "sub"), None),
            P(("grp", "pool"), ("head", "sub"), None),
        ),
        check_vma=False,
    )
```
